32 devices in a mesh: dp: 8 (over z, x), blk: 4 (over y, core).
Axes of the slice: x: 2, y: 2, z: 4, core: 2. Of those that a mesh axis runs over, the one named last changes fastest.
Arguments:
- embeddings: bfloat16 [8192, 768], P(('dp', 'blk')), may hold values from -6 to 6
- point_group: int32 [8192, 1], P(('dp', 'blk')), may hold values from 0 to 7; in each aligned block of 256 rows (0 to 255, 256 to 511, ...) at most 64 rows name the same one
- point_cluster: int32 [8192], P(('dp', 'blk')), may hold values from 0 to 31
- point_order: int32 [8192], P(('dp', 'blk')), may hold values from 0 to 8191, each once
Outputs:
- nearest: float32 [8192], P(('dp', 'blk'))
The draws below stay inside these ranges and needn't reach their ends.
Inputs may be any that keep to these rules, and one draw needn't show every extreme that they name: `point_group`: among the rows of one device at most 64 name the same group, a bound that some blocks reach. `point_order`: every value appears once.
All inputs are finite; a program needn't handle non-finite values.
Results may differ from the reference program's by a relative error of at most 0.00077.
Values may be sent and summed in bfloat16 or wider, within the bound.
A program may use at most 64 MiB of HBM per device.

```python
import math
import jax
import jax.numpy as jnp
import numpy as np
from jax import lax

D = 768
PTS_DEV = 256
CLG = 32
POINTS = 8192
CAP = 64
GROUP_ROWS = 2048
N_DP = 8


def touch_ends(array, own_key, least, high):
    spot = [jax.random.randint(jax.random.fold_in(own_key, axis), (), 0, length) for axis, length in enumerate(array.shape)]
    main_axis = array.shape.index(max(array.shape))
    next_to = spot[:main_axis] + [(spot[main_axis] + 1) % array.shape[main_axis]] + spot[main_axis + 1:]
    return array.at[tuple(spot)].set(least).at[tuple(next_to)].set(high)


def levels(rng, dims, pieces, smallest, top_value):
    gain = 1.0
    for axis_at, shards_of in pieces:
        steps = jax.random.uniform(jax.random.fold_in(jax.random.fold_in(rng, 6), axis_at), (shards_of,), jnp.float32, smallest / len(pieces), top_value / len(pieces))
        gain = gain * jnp.repeat(jnp.exp(steps), dims[axis_at] // shards_of).reshape((-1,) + (1,) * (len(dims) - 1 - axis_at))
    return gain


def assign_block(rng, own, number, rows, count, top, bound, slope):
    ranking = jax.random.permutation(rng, count)
    crowded, common = portions_of(count, rows * top, bound, slope, True), portions_of(count, rows * top, bound, slope, False)
    places = jnp.arange(count)

    def named(sizes, offset_by):
        used = int((sizes > 0).sum())
        fixed = max(1, used // 4)
        moved = fixed + (places - fixed + offset_by * (used - fixed)) % max(1, count - fixed)
        return jnp.zeros((count,), jnp.int32).at[ranking[jnp.where(places < fixed, places, moved)]].set(jnp.asarray(sizes, jnp.int32))

    sizes = jnp.where(number % 4 == 0, named(crowded, number // 4), named(common, number - number // 4 - 1))
    mixed = jax.random.permutation(jax.random.fold_in(own, 3), count)
    donor, receiver = mixed[0:count // 2 * 2:2], mixed[1:count // 2 * 2:2]
    slack = jnp.minimum(sizes[donor] - 1, bound - sizes[receiver]) // 2
    slack = jnp.where((donor == ranking[0]) | (receiver == ranking[0]) | (sizes[receiver] == 0), 0, jnp.maximum(slack, 0))
    moved = jax.random.randint(jax.random.fold_in(own, 4), (count // 2,), 0, 1 << 20) % (slack + 1)
    sizes = sizes.at[donor].add(-moved).at[receiver].add(moved)
    items = jnp.searchsorted(jnp.cumsum(sizes), jnp.arange(rows * top), side="right").astype(jnp.int32)
    grid = items.reshape(top, rows).T
    grid = grid[jax.random.permutation(jax.random.fold_in(own, 1), rows)]
    offset_by = jax.random.randint(jax.random.fold_in(own, 2), (rows, 1), 0, top)
    return jnp.take_along_axis(grid, (jnp.arange(top)[None, :] + offset_by) % top, axis=1)


def portions_of(number_of, total, reach, skew, full):
    loads = [(1 << 20) // math.isqrt(rank ** skew) + 1 for rank in range(1, number_of + 1)]
    largest = reach if full else min(reach, max(-(-total // number_of), total * loads[0] // sum(loads)))
    least = 1 if total - largest >= number_of - 1 else 0
    given, spare = [largest] + [least] * (number_of - 1), total - largest - least * (number_of - 1)
    while spare > 0:
        candidates = [i for i in range(1, number_of) if given[i] < largest] or [i for i in range(1, number_of) if given[i] < reach]
        mass, budget = sum([loads[i] for i in candidates]), spare
        for i in candidates:
            extra = min(reach - given[i], max(1, budget * loads[i] // mass), spare)
            given[i] = given[i] + extra
            spare = spare - extra
    return np.array(given)


def scatter_about(own_key, shape, scale, reach, split=(), held_as=jnp.bfloat16):
    drawn = jax.random.normal(own_key, shape, jnp.float32) * scale
    if len(split) > 0:
        drawn = levels(own_key, shape, split, -0.22, 0.18) * drawn
    return jnp.clip(drawn, min=-reach, max=reach).astype(held_as)


def setup_inputs(seed: int = 0) -> dict:
    key_of = jax.random.split(jax.random.key(seed), 5)
    embeddings = scatter_about(key_of[0], (POINTS, D), 1.0, 6.0, ((0, 32),))
    point_group_keys = jax.random.split(jax.random.fold_in(key_of[1], 1), POINTS // PTS_DEV)
    point_group_turns = jax.random.permutation(jax.random.fold_in(key_of[1], 3), POINTS // PTS_DEV)
    point_group = jax.vmap(lambda own, number: assign_block(jax.random.fold_in(key_of[1], 2), own, number, PTS_DEV, N_DP, 1, CAP, 1))(point_group_keys, point_group_turns).reshape((POINTS, 1))
    point_cluster = touch_ends(jax.random.randint(key_of[2], (POINTS,), 0, CLG), jax.random.fold_in(key_of[2], 1), 0, CLG - 1).astype(jnp.int32)
    point_order = jax.random.permutation(key_of[3], POINTS).astype(jnp.int32)
    return dict(embeddings=embeddings, point_group=point_group, point_cluster=point_cluster, point_order=point_order)


def reference(embeddings, point_group, point_cluster, point_order):
    values = embeddings.astype(jnp.float32)
    scale = lax.rsqrt(lax.optimization_barrier(jnp.mean(values * values, axis=1, keepdims=True)) + 1e-06)
    unit = (values * scale * D ** (-0.5)).astype(jnp.bfloat16)
    group = point_group[:, 0].astype(jnp.int32)
    labels = group * CLG + point_cluster.astype(jnp.int32)
    order = point_order.astype(jnp.int32)
    perm = jnp.argsort(group, stable=True).astype(jnp.int32)
    member = (group[:, None] == jnp.arange(N_DP, dtype=jnp.int32)[None, :]).astype(jnp.int32)
    counts = lax.optimization_barrier(jnp.sum(member, axis=0)).astype(jnp.int32)
    starts = (jnp.cumsum(counts) - counts).astype(jnp.int32)
    pad_unit = jnp.concatenate([unit[perm], jnp.zeros((GROUP_ROWS, D), jnp.bfloat16)], axis=0)
    pad_labels = jnp.concatenate([labels[perm], jnp.full((GROUP_ROWS,), -1, jnp.int32)], axis=0)
    pad_order = jnp.concatenate([order[perm], jnp.zeros((GROUP_ROWS,), jnp.int32)], axis=0)

    def one_group(index):
        first = starts[index].astype(jnp.int32)
        rows = lax.dynamic_slice_in_dim(pad_unit, first, GROUP_ROWS, 0).astype(jnp.float32)
        group_labels = lax.dynamic_slice_in_dim(pad_labels, first, GROUP_ROWS, 0)
        group_order = lax.dynamic_slice_in_dim(pad_order, first, GROUP_ROWS, 0)
        valid = jnp.arange(GROUP_ROWS, dtype=jnp.int32) < counts[index]
        group_labels = jnp.where(valid, group_labels, -1)
        scores = jnp.dot(rows, rows.T, precision=lax.Precision.HIGHEST, preferred_element_type=jnp.float32)
        mask = (group_labels[:, None] == group_labels[None, :]) & (group_order[None, :] < group_order[:, None]) & valid[:, None]
        best = lax.optimization_barrier(jnp.max(jnp.where(mask, scores, -2.0), axis=1))
        return jnp.where(best > -1.5, best, -1.0)
    table = lax.map(one_group, jnp.arange(N_DP, dtype=jnp.int32))
    sorted_group = group[perm]
    position = jnp.arange(POINTS, dtype=jnp.int32) - starts[sorted_group]
    sorted_best = table[sorted_group, position]
    return jnp.zeros((POINTS,), jnp.float32).at[perm].set(sorted_best)
```

```python
import functools

import jax
import jax.numpy as jnp
from jax import lax
from jax.experimental import pallas as pl
from jax.experimental.pallas import tpu as pltpu
from jax.sharding import PartitionSpec as P

CLG = 32
LANES = 128
MESH = pl.DeviceIdType.MESH
NT = (((1,), (1,)), ((), ()))


def flip(index, mask):
    out = index
    bit = 1
    while bit <= mask:
        if mask & bit:
            digit = lax.rem(lax.div(index, jnp.int32(bit)), jnp.int32(2))
            out = out + bit * (1 - 2 * digit)
        bit *= 2
    return out


def kernel(groups, total, order, emb_ref, ids_ref, out_ref, send, keys, msend, meta, kmeta, res, back,
           s1, r1, sm, rm, sy, ry, sc, rc, sd, rd, smx, rmx, sb, rb):
    points, width = emb_ref.shape
    cap = 2 * points // groups
    slots = groups * cap
    per = LANES // cap
    tiles = slots // LANES
    me = lax.axis_index("dp")
    own = lax.axis_index("blk")
    across = {"blk": flip(own, 2)}
    beside = {"blk": flip(own, 1)}
    partner = [None] + [{"dp": flip(me, k)} for k in range(1, groups)]

    barrier = pltpu.get_barrier_semaphore()
    for who in partner[1:] + [across, beside]:
        pl.semaphore_signal(barrier, inc=1, device_id=who, device_id_type=MESH)

    def remote(src, dst, ssem, rsem, who):
        return pltpu.make_async_remote_copy(
            src_ref=src, dst_ref=dst, send_sem=ssem, recv_sem=rsem, device_id=who, device_id_type=MESH
        )

    group = ids_ref[0:1, :]
    combined = ids_ref[1:2, :] * total + ids_ref[2:3, :] + 1
    relative = jnp.bitwise_xor(group, me)
    member = lax.broadcasted_iota(jnp.int32, (groups, points), 0) == relative
    member_f = jnp.where(member, 1.0, 0.0)
    earlier = lax.broadcasted_iota(jnp.int32, (points, points), 0) < lax.broadcasted_iota(
        jnp.int32, (points, points), 1
    )
    before = jnp.dot(
        member_f.astype(jnp.bfloat16),
        jnp.where(earlier, 1.0, 0.0).astype(jnp.bfloat16),
        preferred_element_type=jnp.float32,
    )
    rank = jnp.sum(before * member_f, axis=0, keepdims=True).astype(jnp.int32)
    target = relative * cap + rank

    digits = jnp.concatenate(
        [combined & 127, (combined >> 7) & 127, combined >> 14, jnp.zeros((5, points), jnp.int32)], axis=0
    ).astype(jnp.float32).astype(jnp.bfloat16)
    lane_slot = lax.broadcasted_iota(jnp.int32, (LANES, points), 0) & (cap - 1)
    local_target = target & (cap - 1)
    same_rank = lane_slot == local_target
    for k in range(groups):
        pick = jnp.where(same_rank & (relative == k), 1.0, 0.0).astype(jnp.bfloat16)
        got = lax.dot_general(digits, pick, NT, preferred_element_type=jnp.float32)
        row = got[0:1, :] + 128.0 * got[1:2, :] + 16384.0 * got[2:3, :]
        row = jnp.broadcast_to(row.astype(jnp.int32), (8, LANES))
        if k == 0:
            meta[0, 0] = row
        else:
            msend[k] = row

    values = emb_ref[...].astype(jnp.float32)
    scale = lax.rsqrt(jnp.mean(values * values, axis=1, keepdims=True) + 1e-06)
    unit = (values * scale * width ** (-0.5)).astype(jnp.bfloat16)

    pl.semaphore_wait(barrier, groups + 1)

    started = []
    meta_copies = [None] * groups
    for k in order:
        meta_copies[k] = remote(msend.at[k], meta.at[0, k], sm.at[k], rm.at[k], partner[k])
        meta_copies[k].start()

    first = [None] * groups
    over_y = [None] * groups
    over_c = [None] * groups
    diag = [None] * groups

    def forward(k):
        over_y[k] = remote(keys.at[0, k], keys.at[2, k], sy.at[k], ry.at[k], across)
        over_y[k].start()
        over_c[k] = remote(keys.at[0, k], keys.at[1, k], sc.at[k], rc.at[k], beside)
        over_c[k].start()

    def onward(k):
        over_y[k].wait_recv()
        diag[k] = remote(keys.at[2, k], keys.at[3, k], sd.at[k], rd.at[k], beside)
        diag[k].start()

    slot_rows = lax.broadcasted_iota(jnp.int32, (cap, points), 0)
    for k in [order[0], 0] + list(order[1:]):
        place = jnp.where(slot_rows + k * cap == target, 1.0, 0.0).astype(jnp.bfloat16)
        rows = jnp.dot(place, unit, preferred_element_type=jnp.float32).astype(jnp.bfloat16)
        if k == 0:
            keys[0, 0] = rows
            forward(0)
        else:
            send[k] = rows
            first[k] = remote(send.at[k], keys.at[0, k], s1.at[k], r1.at[k], partner[k])
            first[k].start()

    def key_tiles(r):
        lane_block = lax.broadcasted_iota(jnp.int32, (1, LANES), 1) // cap
        rows = []
        for t in range(tiles):
            row = meta[r, t * per][0:1, :]
            for j in range(1, per):
                row = jnp.where(lane_block == j, meta[r, t * per + j][0:1, :], row)
            rows.append(row)
            kmeta[r, t] = jnp.broadcast_to(row, (LANES, LANES)).T
        return rows

    for k in order:
        meta_copies[k].wait_recv()
    meta_y = remote(meta.at[0], meta.at[2], smx.at[0], rmx.at[0], across)
    meta_y.start()
    meta_c = remote(meta.at[0], meta.at[1], smx.at[1], rmx.at[1], beside)
    meta_c.start()
    query = jnp.concatenate(key_tiles(0), axis=1)
    floor = (query - 1) & (-total)

    arrive = sorted(order, key=lambda k: (k.bit_length(), k))
    queue = [0]
    for k in arrive:
        first[k].wait_recv()
        forward(k)
        onward(queue.pop(0))
        queue.append(k)
        if k == 1:
            meta_y.wait_recv()
            meta_d = remote(meta.at[2], meta.at[3], smx.at[2], rmx.at[2], beside)
            meta_d.start()
    meta_c.wait_recv()
    key_tiles(1)
    key_tiles(2)
    meta_d.wait_recv()
    key_tiles(3)

    queries = keys[0].reshape(slots, width)
    half = groups // 2

    def visit(best, r, h):
        block = keys[r, h * half:(h + 1) * half].reshape(half * cap, width)
        scores = lax.dot_general(block, queries, NT, preferred_element_type=jnp.float32)
        for t in range(tiles // 2):
            mine = kmeta[r, h * (tiles // 2) + t]
            mine = jnp.concatenate([mine] * tiles, axis=1)
            part = jnp.where((mine < query) & (mine > floor), scores[t * LANES:(t + 1) * LANES], -2.0)
            best = jnp.maximum(best, jnp.max(part.reshape(LANES // 8, 8, slots), axis=0))
        return best

    best = jnp.full((8, slots), -2.0, jnp.float32)
    best = visit(best, 0, 0)
    onward(queue.pop(0))
    for r in (0, 1, 2, 3):
        for h in (0, 1):
            if r == 0 and h == 0:
                continue
            if r == 1 or r == 3:
                for k in range(h * half, (h + 1) * half):
                    (over_c if r == 1 else diag)[k].wait_recv()
            best = visit(best, r, h)
    best = jnp.max(best, axis=0, keepdims=True)
    answer = jnp.broadcast_to(jnp.where(best > -1.5, best, -1.0), (8, slots))
    for t in range(tiles):
        res[t] = answer[:, t * LANES:(t + 1) * LANES]
    back[0] = res[0]
    replies = [None] * groups
    for k in order:
        replies[k] = remote(res.at[k // per], back.at[k], sb.at[k], rb.at[k], partner[k])
        replies[k].start()

    for k in range(groups):
        over_y[k].wait_send()
        over_c[k].wait_send()
        diag[k].wait_send()
        if k:
            first[k].wait_send()
            meta_copies[k].wait_send()
    meta_y.wait_send()
    meta_c.wait_send()
    meta_d.wait_send()

    lane_block = lax.broadcasted_iota(jnp.int32, (1, LANES), 1) // cap
    nearest = jnp.full((1, points), -2.0, jnp.float32)
    slot_iota = lax.broadcasted_iota(jnp.int32, (LANES, points), 0)
    for t in range(tiles):
        for j in range(per):
            if t * per + j:
                replies[t * per + j].wait_recv()
        row = back[t * per][0:1, :]
        for j in range(1, per):
            row = jnp.where(lane_block == j, back[t * per + j][0:1, :], row)
        column = jnp.broadcast_to(row, (LANES, LANES)).T
        column = jnp.concatenate([column] * (points // LANES), axis=1)
        hit = jnp.where(slot_iota + t * LANES == target, column, -2.0)
        nearest = jnp.maximum(nearest, jnp.max(hit, axis=0, keepdims=True))
    out_ref[...] = nearest
    for k in order:
        replies[k].wait_send()


def body(total, embeddings, point_group, point_cluster, point_order):
    groups = lax.axis_size("dp")
    blocks = lax.axis_size("blk")
    points, width = embeddings.shape
    cap = 2 * points // groups
    slots = groups * cap
    ids = jnp.stack([point_group[:, 0], point_cluster, point_order])
    order = [k for k in range(groups // 2, groups)] + [k for k in range(1, groups // 2)]
    dma = pltpu.SemaphoreType.DMA
    out = pl.pallas_call(
        functools.partial(kernel, groups, total, order),
        out_shape=jax.ShapeDtypeStruct((1, points), jnp.float32),
        in_specs=[pl.BlockSpec(memory_space=pltpu.VMEM)] * 2,
        out_specs=pl.BlockSpec(memory_space=pltpu.VMEM),
        scratch_shapes=[
            pltpu.VMEM((groups, cap, width), jnp.bfloat16),
            pltpu.VMEM((blocks, groups, cap, width), jnp.bfloat16),
            pltpu.VMEM((groups, 8, LANES), jnp.int32),
            pltpu.VMEM((blocks, groups, 8, LANES), jnp.int32),
            pltpu.VMEM((blocks, slots // LANES, LANES, LANES), jnp.int32),
            pltpu.VMEM((slots // LANES, 8, LANES), jnp.float32),
            pltpu.VMEM((groups, 8, LANES), jnp.float32),
        ]
        + [dma((groups,))] * 10
        + [dma((3,))] * 2
        + [dma((groups,))] * 2,
        compiler_params=pltpu.CompilerParams(
            collective_id=0, has_side_effects=True, vmem_limit_bytes=48 * 1024 * 1024
        ),
        cost_estimate=pl.CostEstimate(
            flops=2 * slots * slots * blocks * width, bytes_accessed=points * width * 2, transcendentals=points
        ),
    )(embeddings, ids)
    return out.reshape(points)


def solution(mesh):
    in_specs = (P(("dp", "blk"), None), P(("dp", "blk"), None), P(("dp", "blk")), P(("dp", "blk")))
    out_specs = P(("dp", "blk"))

    def run(embeddings, point_group, point_cluster, point_order):
        inner = functools.partial(body, embeddings.shape[0])
        return jax.shard_map(inner, mesh=mesh, in_specs=in_specs, out_specs=out_specs, check_vma=False)(
            embeddings, point_group, point_cluster, point_order
        )

    return run
```

```python
import functools

import jax
import jax.numpy as jnp
from jax import lax
from jax.experimental import pallas as pl
from jax.experimental.pallas import tpu as pltpu
from jax.sharding import PartitionSpec as P

CLG = 32
LANES = 128
MESH = pl.DeviceIdType.MESH
NT = (((1,), (1,)), ((), ()))


def flip(index, mask):
    out = index
    bit = 1
    while bit <= mask:
        if mask & bit:
            digit = lax.rem(lax.div(index, jnp.int32(bit)), jnp.int32(2))
            out = out + bit * (1 - 2 * digit)
        bit *= 2
    return out


def kernel(groups, total, order, emb_hbm, group_hbm, cluster_hbm, order_hbm, out_ref, emb_ref, ids, fetched,
           send, keys, msend, meta, kmeta, res, back, s1, r1, sm, rm, sy, ry, sc, rc, sd, rd, smx, rmx, sb, rb):
    points, width = emb_ref.shape
    cap = 2 * points // groups
    slots = groups * cap
    per = LANES // cap
    tiles = slots // LANES
    me = lax.axis_index("dp")
    own = lax.axis_index("blk")
    across = {"blk": flip(own, 2)}
    beside = {"blk": flip(own, 1)}
    partner = [None] + [{"dp": flip(me, k)} for k in range(1, groups)]

    fetches = [
        pltpu.make_async_copy(group_hbm, ids.at[0], fetched.at[0]),
        pltpu.make_async_copy(cluster_hbm, ids.at[1], fetched.at[1]),
        pltpu.make_async_copy(order_hbm, ids.at[2], fetched.at[2]),
        pltpu.make_async_copy(emb_hbm, emb_ref, fetched.at[3]),
    ]
    for fetch in fetches:
        fetch.start()

    barrier = pltpu.get_barrier_semaphore()
    for who in partner[1:] + [across, beside]:
        pl.semaphore_signal(barrier, inc=1, device_id=who, device_id_type=MESH)

    def remote(src, dst, ssem, rsem, who):
        return pltpu.make_async_remote_copy(
            src_ref=src, dst_ref=dst, send_sem=ssem, recv_sem=rsem, device_id=who, device_id_type=MESH
        )

    for fetch in fetches[:3]:
        fetch.wait()
    group = ids[0]
    combined = ids[1] * total + ids[2] + 1
    relative = jnp.bitwise_xor(group, me)
    member = lax.broadcasted_iota(jnp.int32, (groups, points), 0) == relative
    member_f = jnp.where(member, 1.0, 0.0)
    earlier = lax.broadcasted_iota(jnp.int32, (points, points), 0) < lax.broadcasted_iota(
        jnp.int32, (points, points), 1
    )
    before = jnp.dot(
        member_f.astype(jnp.bfloat16),
        jnp.where(earlier, 1.0, 0.0).astype(jnp.bfloat16),
        preferred_element_type=jnp.float32,
    )
    rank = jnp.sum(before * member_f, axis=0, keepdims=True).astype(jnp.int32)
    target = relative * cap + rank

    digits = jnp.concatenate(
        [combined & 127, (combined >> 7) & 127, combined >> 14, jnp.zeros((5, points), jnp.int32)], axis=0
    ).astype(jnp.float32).astype(jnp.bfloat16)
    lane_slot = lax.broadcasted_iota(jnp.int32, (LANES, points), 0) & (cap - 1)
    local_target = target & (cap - 1)
    same_rank = lane_slot == local_target
    for k in range(groups):
        pick = jnp.where(same_rank & (relative == k), 1.0, 0.0).astype(jnp.bfloat16)
        got = lax.dot_general(digits, pick, NT, preferred_element_type=jnp.float32)
        row = got[0:1, :] + 128.0 * got[1:2, :] + 16384.0 * got[2:3, :]
        row = jnp.broadcast_to(row.astype(jnp.int32), (8, LANES))
        if k == 0:
            meta[0, 0] = row
        else:
            msend[k] = row

    fetches[3].wait()
    values = emb_ref[...].astype(jnp.float32)
    scale = lax.rsqrt(jnp.mean(values * values, axis=1, keepdims=True) + 1e-06)
    unit = (values * scale * width ** (-0.5)).astype(jnp.bfloat16)

    pl.semaphore_wait(barrier, groups + 1)

    started = []
    meta_copies = [None] * groups
    for k in order:
        meta_copies[k] = remote(msend.at[k], meta.at[0, k], sm.at[k], rm.at[k], partner[k])
        meta_copies[k].start()

    first = [None] * groups
    over_y = [None] * groups
    over_c = [None] * groups
    diag = [None] * groups

    def forward(k):
        over_y[k] = remote(keys.at[0, k], keys.at[2, k], sy.at[k], ry.at[k], across)
        over_y[k].start()
        over_c[k] = remote(keys.at[0, k], keys.at[1, k], sc.at[k], rc.at[k], beside)
        over_c[k].start()

    def onward(k):
        over_y[k].wait_recv()
        diag[k] = remote(keys.at[2, k], keys.at[3, k], sd.at[k], rd.at[k], beside)
        diag[k].start()

    slot_rows = lax.broadcasted_iota(jnp.int32, (cap, points), 0)
    for k in [order[0], 0] + list(order[1:]):
        place = jnp.where(slot_rows + k * cap == target, 1.0, 0.0).astype(jnp.bfloat16)
        rows = jnp.dot(place, unit, preferred_element_type=jnp.float32).astype(jnp.bfloat16)
        if k == 0:
            keys[0, 0] = rows
            forward(0)
        else:
            send[k] = rows
            first[k] = remote(send.at[k], keys.at[0, k], s1.at[k], r1.at[k], partner[k])
            first[k].start()

    def key_tiles(r):
        lane_block = lax.broadcasted_iota(jnp.int32, (1, LANES), 1) // cap
        rows = []
        for t in range(tiles):
            row = meta[r, t * per][0:1, :]
            for j in range(1, per):
                row = jnp.where(lane_block == j, meta[r, t * per + j][0:1, :], row)
            rows.append(row)
            kmeta[r, t] = jnp.broadcast_to(row, (LANES, LANES)).T
        return rows

    for k in order:
        meta_copies[k].wait_recv()
    meta_y = remote(meta.at[0], meta.at[2], smx.at[0], rmx.at[0], across)
    meta_y.start()
    meta_c = remote(meta.at[0], meta.at[1], smx.at[1], rmx.at[1], beside)
    meta_c.start()
    query = jnp.concatenate(key_tiles(0), axis=1)
    floor = (query - 1) & (-total)

    queue = [0]
    for k in order:
        first[k].wait_recv()
        forward(k)
        onward(queue.pop(0))
        queue.append(k)
        if k == order[1]:
            meta_y.wait_recv()
            meta_d = remote(meta.at[2], meta.at[3], smx.at[2], rmx.at[2], beside)
            meta_d.start()
    meta_c.wait_recv()
    key_tiles(1)
    key_tiles(2)
    meta_d.wait_recv()
    key_tiles(3)

    queries = keys[0].reshape(slots, width)
    half = groups // 2

    def visit(best, r, h):
        block = keys[r, h * half:(h + 1) * half].reshape(half * cap, width)
        scores = lax.dot_general(block, queries, NT, preferred_element_type=jnp.float32)
        for t in range(tiles // 2):
            mine = kmeta[r, h * (tiles // 2) + t]
            mine = jnp.concatenate([mine] * tiles, axis=1)
            part = jnp.where((mine < query) & (mine > floor), scores[t * LANES:(t + 1) * LANES], -2.0)
            best = jnp.maximum(best, jnp.max(part.reshape(LANES // 8, 8, slots), axis=0))
        return best

    best = jnp.full((8, slots), -2.0, jnp.float32)
    best = visit(best, 0, 0)
    onward(queue.pop(0))
    for r in (0, 1, 2, 3):
        for h in (0, 1):
            if r == 0 and h == 0:
                continue
            if r == 1 or r == 3:
                for k in range(h * half, (h + 1) * half):
                    (over_c if r == 1 else diag)[k].wait_recv()
            best = visit(best, r, h)
    best = jnp.max(best, axis=0, keepdims=True)
    answer = jnp.broadcast_to(jnp.where(best > -1.5, best, -1.0), (8, slots))
    for t in range(tiles):
        res[t] = answer[:, t * LANES:(t + 1) * LANES]
    back[0] = res[0]
    replies = [None] * groups
    for k in order:
        replies[k] = remote(res.at[k // per], back.at[k], sb.at[k], rb.at[k], partner[k])
        replies[k].start()

    for k in range(groups):
        over_y[k].wait_send()
        over_c[k].wait_send()
        diag[k].wait_send()
        if k:
            first[k].wait_send()
            meta_copies[k].wait_send()
    meta_y.wait_send()
    meta_c.wait_send()
    meta_d.wait_send()

    lane_block = lax.broadcasted_iota(jnp.int32, (1, LANES), 1) // cap
    nearest = jnp.full((1, points), -2.0, jnp.float32)
    slot_iota = lax.broadcasted_iota(jnp.int32, (LANES, points), 0)
    for t in range(tiles):
        for j in range(per):
            if t * per + j:
                replies[t * per + j].wait_recv()
        row = back[t * per][0:1, :]
        for j in range(1, per):
            row = jnp.where(lane_block == j, back[t * per + j][0:1, :], row)
        column = jnp.broadcast_to(row, (LANES, LANES)).T
        column = jnp.concatenate([column] * (points // LANES), axis=1)
        hit = jnp.where(slot_iota + t * LANES == target, column, -2.0)
        nearest = jnp.maximum(nearest, jnp.max(hit, axis=0, keepdims=True))
    out_ref[...] = nearest
    for k in order:
        replies[k].wait_send()


def body(total, embeddings, point_group, point_cluster, point_order):
    groups = lax.axis_size("dp")
    blocks = lax.axis_size("blk")
    points, width = embeddings.shape
    cap = 2 * points // groups
    slots = groups * cap
    near, far = list(range(1, groups // 2)), list(range(groups // 2, groups))
    order = [k for pair in zip(near, far) for k in pair] + far[len(near):]
    dma = pltpu.SemaphoreType.DMA
    out = pl.pallas_call(
        functools.partial(kernel, groups, total, order),
        out_shape=jax.ShapeDtypeStruct((1, points), jnp.float32),
        in_specs=[pl.BlockSpec(memory_space=pl.ANY)] * 4,
        out_specs=pl.BlockSpec(memory_space=pltpu.VMEM),
        scratch_shapes=[
            pltpu.VMEM((points, width), jnp.bfloat16),
            pltpu.VMEM((3, 1, points), jnp.int32),
            dma((4,)),
            pltpu.VMEM((groups, cap, width), jnp.bfloat16),
            pltpu.VMEM((blocks, groups, cap, width), jnp.bfloat16),
            pltpu.VMEM((groups, 8, LANES), jnp.int32),
            pltpu.VMEM((blocks, groups, 8, LANES), jnp.int32),
            pltpu.VMEM((blocks, slots // LANES, LANES, LANES), jnp.int32),
            pltpu.VMEM((slots // LANES, 8, LANES), jnp.float32),
            pltpu.VMEM((groups, 8, LANES), jnp.float32),
        ]
        + [dma((groups,))] * 10
        + [dma((3,))] * 2
        + [dma((groups,))] * 2,
        compiler_params=pltpu.CompilerParams(
            collective_id=0, has_side_effects=True, vmem_limit_bytes=64 * 1024 * 1024 - 65536
        ),
        cost_estimate=pl.CostEstimate(
            flops=2 * slots * slots * blocks * width, bytes_accessed=points * width * 2, transcendentals=points
        ),
    )(embeddings, point_group.reshape(1, points), point_cluster.reshape(1, points), point_order.reshape(1, points))
    return out.reshape(points)


def solution(mesh):
    in_specs = (P(("dp", "blk"), None), P(("dp", "blk"), None), P(("dp", "blk")), P(("dp", "blk")))
    out_specs = P(("dp", "blk"))

    def run(embeddings, point_group, point_cluster, point_order):
        inner = functools.partial(body, embeddings.shape[0])
        return jax.shard_map(inner, mesh=mesh, in_specs=in_specs, out_specs=out_specs, check_vma=False)(
            embeddings, point_group, point_cluster, point_order
        )

    return run
```

```python
import functools

import jax
import jax.numpy as jnp
from jax import lax
from jax.experimental import pallas as pl
from jax.experimental.pallas import tpu as pltpu
from jax.sharding import PartitionSpec as P

CLG = 32
LANES = 128
MESH = pl.DeviceIdType.MESH
NT = (((1,), (1,)), ((), ()))


def flip(index, mask):
    out = index
    bit = 1
    while bit <= mask:
        if mask & bit:
            digit = lax.rem(lax.div(index, jnp.int32(bit)), jnp.int32(2))
            out = out + bit * (1 - 2 * digit)
        bit *= 2
    return out


def kernel(groups, total, order, emb_hbm, group_hbm, cluster_hbm, order_hbm, out_ref, emb_ref, ids, fetched,
           send, keys, msend, meta, kmeta, res, back, s1, r1, sm, rm, sy, ry, sc, rc, sd, rd, smx, rmx, sb, rb):
    points, width = emb_ref.shape
    cap = 2 * points // groups
    slots = groups * cap
    per = LANES // cap
    tiles = slots // LANES
    me = lax.axis_index("dp")
    own = lax.axis_index("blk")
    across = {"blk": flip(own, 2)}
    beside = {"blk": flip(own, 1)}
    partner = [None] + [{"dp": flip(me, k)} for k in range(1, groups)]

    fetches = [
        pltpu.make_async_copy(group_hbm, ids.at[0], fetched.at[0]),
        pltpu.make_async_copy(cluster_hbm, ids.at[1], fetched.at[1]),
        pltpu.make_async_copy(order_hbm, ids.at[2], fetched.at[2]),
        pltpu.make_async_copy(emb_hbm, emb_ref, fetched.at[3]),
    ]
    for fetch in fetches:
        fetch.start()

    barrier = pltpu.get_barrier_semaphore()
    for who in partner[1:] + [across, beside]:
        pl.semaphore_signal(barrier, inc=1, device_id=who, device_id_type=MESH)

    def remote(src, dst, ssem, rsem, who):
        return pltpu.make_async_remote_copy(
            src_ref=src, dst_ref=dst, send_sem=ssem, recv_sem=rsem, device_id=who, device_id_type=MESH
        )

    for fetch in fetches[:3]:
        fetch.wait()
    group = ids[0]
    combined = ids[1] * total + ids[2] + 1
    relative = jnp.bitwise_xor(group, me)
    member = lax.broadcasted_iota(jnp.int32, (groups, points), 0) == relative
    member_f = jnp.where(member, 1.0, 0.0)
    earlier = lax.broadcasted_iota(jnp.int32, (points, points), 0) < lax.broadcasted_iota(
        jnp.int32, (points, points), 1
    )
    before = jnp.dot(
        member_f.astype(jnp.bfloat16),
        jnp.where(earlier, 1.0, 0.0).astype(jnp.bfloat16),
        preferred_element_type=jnp.float32,
    )
    rank = jnp.sum(before * member_f, axis=0, keepdims=True).astype(jnp.int32)
    target = relative * cap + rank

    digits = jnp.concatenate(
        [combined & 127, (combined >> 7) & 127, combined >> 14, jnp.zeros((5, points), jnp.int32)], axis=0
    ).astype(jnp.float32).astype(jnp.bfloat16)
    lane_slot = lax.broadcasted_iota(jnp.int32, (LANES, points), 0) & (cap - 1)
    local_target = target & (cap - 1)
    same_rank = lane_slot == local_target
    for k in range(groups):
        pick = jnp.where(same_rank & (relative == k), 1.0, 0.0).astype(jnp.bfloat16)
        got = lax.dot_general(digits, pick, NT, preferred_element_type=jnp.float32)
        row = got[0:1, :] + 128.0 * got[1:2, :] + 16384.0 * got[2:3, :]
        row = jnp.broadcast_to(row.astype(jnp.int32), (8, LANES))
        if k == 0:
            meta[0, 0] = row
        else:
            msend[k] = row

    fetches[3].wait()
    values = emb_ref[...].astype(jnp.float32)
    scale = lax.rsqrt(jnp.mean(values * values, axis=1, keepdims=True) + 1e-06)
    unit = (values * scale * width ** (-0.5)).astype(jnp.bfloat16)

    pl.semaphore_wait(barrier, groups + 1)

    started = []
    meta_copies = [None] * groups
    for k in order:
        meta_copies[k] = remote(msend.at[k], meta.at[0, k], sm.at[k], rm.at[k], partner[k])
        meta_copies[k].start()

    first = [None] * groups
    over_y = [None] * groups
    over_c = [None] * groups
    diag = [None] * groups

    def forward(k):
        over_y[k] = remote(keys.at[0, k], keys.at[2, k], sy.at[k], ry.at[k], across)
        over_y[k].start()
        over_c[k] = remote(keys.at[0, k], keys.at[1, k], sc.at[k], rc.at[k], beside)
        over_c[k].start()

    def onward(k):
        over_y[k].wait_recv()
        diag[k] = remote(keys.at[2, k], keys.at[3, k], sd.at[k], rd.at[k], beside)
        diag[k].start()

    slot_rows = lax.broadcasted_iota(jnp.int32, (cap, points), 0)
    window = groups // 4
    held_back = [k for k in order if k >= groups // 2][window:]
    for k in [order[0], 0] + list(order[1:]):
        place = jnp.where(slot_rows + k * cap == target, 1.0, 0.0).astype(jnp.bfloat16)
        rows = jnp.dot(place, unit, preferred_element_type=jnp.float32).astype(jnp.bfloat16)
        if k == 0:
            keys[0, 0] = rows
            forward(0)
        else:
            send[k] = rows
            first[k] = remote(send.at[k], keys.at[0, k], s1.at[k], r1.at[k], partner[k])
            if k not in held_back:
                first[k].start()

    def key_tiles(r):
        lane_block = lax.broadcasted_iota(jnp.int32, (1, LANES), 1) // cap
        rows = []
        for t in range(tiles):
            row = meta[r, t * per][0:1, :]
            for j in range(1, per):
                row = jnp.where(lane_block == j, meta[r, t * per + j][0:1, :], row)
            rows.append(row)
            kmeta[r, t] = jnp.broadcast_to(row, (LANES, LANES)).T
        return rows

    for k in order:
        meta_copies[k].wait_recv()
    meta_y = remote(meta.at[0], meta.at[2], smx.at[0], rmx.at[0], across)
    meta_y.start()
    meta_c = remote(meta.at[0], meta.at[1], smx.at[1], rmx.at[1], beside)
    meta_c.start()
    query = jnp.concatenate(key_tiles(0), axis=1)
    floor = (query - 1) & (-total)

    queue = [0]
    for k in order:
        first[k].wait_recv()
        if k >= groups // 2 and held_back:
            first[held_back.pop(0)].start()
        forward(k)
        onward(queue.pop(0))
        queue.append(k)
        if k == order[1]:
            meta_y.wait_recv()
            meta_d = remote(meta.at[2], meta.at[3], smx.at[2], rmx.at[2], beside)
            meta_d.start()
    meta_c.wait_recv()
    key_tiles(1)
    key_tiles(2)
    meta_d.wait_recv()
    key_tiles(3)

    queries = keys[0].reshape(slots, width)
    half = groups // 2

    def visit(best, r, h):
        block = keys[r, h * half:(h + 1) * half].reshape(half * cap, width)
        scores = lax.dot_general(block, queries, NT, preferred_element_type=jnp.float32)
        for t in range(tiles // 2):
            mine = kmeta[r, h * (tiles // 2) + t]
            mine = jnp.concatenate([mine] * tiles, axis=1)
            part = jnp.where((mine < query) & (mine > floor), scores[t * LANES:(t + 1) * LANES], -2.0)
            best = jnp.maximum(best, jnp.max(part.reshape(LANES // 8, 8, slots), axis=0))
        return best

    best = jnp.full((8, slots), -2.0, jnp.float32)
    best = visit(best, 0, 0)
    onward(queue.pop(0))
    for r in (0, 1, 2, 3):
        for h in (0, 1):
            if r == 0 and h == 0:
                continue
            if r == 1 or r == 3:
                for k in range(h * half, (h + 1) * half):
                    (over_c if r == 1 else diag)[k].wait_recv()
            best = visit(best, r, h)
    best = jnp.max(best, axis=0, keepdims=True)
    answer = jnp.broadcast_to(jnp.where(best > -1.5, best, -1.0), (8, slots))
    for t in range(tiles):
        res[t] = answer[:, t * LANES:(t + 1) * LANES]
    back[0] = res[0]
    replies = [None] * groups
    for k in order:
        replies[k] = remote(res.at[k // per], back.at[k], sb.at[k], rb.at[k], partner[k])
        replies[k].start()

    for k in range(groups):
        over_y[k].wait_send()
        over_c[k].wait_send()
        diag[k].wait_send()
        if k:
            first[k].wait_send()
            meta_copies[k].wait_send()
    meta_y.wait_send()
    meta_c.wait_send()
    meta_d.wait_send()

    lane_block = lax.broadcasted_iota(jnp.int32, (1, LANES), 1) // cap
    nearest = jnp.full((1, points), -2.0, jnp.float32)
    slot_iota = lax.broadcasted_iota(jnp.int32, (LANES, points), 0)
    for t in range(tiles):
        for j in range(per):
            if t * per + j:
                replies[t * per + j].wait_recv()
        row = back[t * per][0:1, :]
        for j in range(1, per):
            row = jnp.where(lane_block == j, back[t * per + j][0:1, :], row)
        column = jnp.broadcast_to(row, (LANES, LANES)).T
        column = jnp.concatenate([column] * (points // LANES), axis=1)
        hit = jnp.where(slot_iota + t * LANES == target, column, -2.0)
        nearest = jnp.maximum(nearest, jnp.max(hit, axis=0, keepdims=True))
    out_ref[...] = nearest.reshape(points)
    for k in order:
        replies[k].wait_send()


def body(total, embeddings, point_group, point_cluster, point_order):
    groups = lax.axis_size("dp")
    blocks = lax.axis_size("blk")
    points, width = embeddings.shape
    cap = 2 * points // groups
    slots = groups * cap
    near, far = list(range(1, groups // 2)), list(range(groups // 2, groups))
    order = [k for pair in zip(near, far) for k in pair] + far[len(near):]
    dma = pltpu.SemaphoreType.DMA
    out = pl.pallas_call(
        functools.partial(kernel, groups, total, order),
        out_shape=jax.ShapeDtypeStruct((points,), jnp.float32),
        in_specs=[pl.BlockSpec(memory_space=pl.ANY)] * 4,
        out_specs=pl.BlockSpec(memory_space=pltpu.VMEM),
        scratch_shapes=[
            pltpu.VMEM((points, width), jnp.bfloat16),
            pltpu.VMEM((3, 1, points), jnp.int32),
            dma((4,)),
            pltpu.VMEM((groups, cap, width), jnp.bfloat16),
            pltpu.VMEM((blocks, groups, cap, width), jnp.bfloat16),
            pltpu.VMEM((groups, 8, LANES), jnp.int32),
            pltpu.VMEM((blocks, groups, 8, LANES), jnp.int32),
            pltpu.VMEM((blocks, slots // LANES, LANES, LANES), jnp.int32),
            pltpu.VMEM((slots // LANES, 8, LANES), jnp.float32),
            pltpu.VMEM((groups, 8, LANES), jnp.float32),
        ]
        + [dma((groups,))] * 10
        + [dma((3,))] * 2
        + [dma((groups,))] * 2,
        compiler_params=pltpu.CompilerParams(
            collective_id=0, has_side_effects=True, vmem_limit_bytes=64 * 1024 * 1024 - 65536
        ),
        cost_estimate=pl.CostEstimate(
            flops=2 * slots * slots * blocks * width, bytes_accessed=points * width * 2, transcendentals=points
        ),
    )(embeddings, point_group.reshape(1, points), point_cluster.reshape(1, points), point_order.reshape(1, points))
    return out


def solution(mesh):
    in_specs = (P(("dp", "blk"), None), P(("dp", "blk"), None), P(("dp", "blk")), P(("dp", "blk")))
    out_specs = P(("dp", "blk"))

    def run(embeddings, point_group, point_cluster, point_order):
        inner = functools.partial(body, embeddings.shape[0])
        return jax.shard_map(inner, mesh=mesh, in_specs=in_specs, out_specs=out_specs, check_vma=False)(
            embeddings, point_group, point_cluster, point_order
        )

    return run
```

```python
import functools

import jax
import jax.numpy as jnp
from jax import lax
from jax.experimental import pallas as pl
from jax.experimental.pallas import tpu as pltpu
from jax.sharding import PartitionSpec as P

CLG = 32
LANES = 128
MESH = pl.DeviceIdType.MESH
NT = (((1,), (1,)), ((), ()))


def flip(index, mask):
    out = index
    bit = 1
    while bit <= mask:
        if mask & bit:
            digit = lax.rem(lax.div(index, jnp.int32(bit)), jnp.int32(2))
            out = out + bit * (1 - 2 * digit)
        bit *= 2
    return out


def kernel(groups, total, perm, first_sends, emb_hbm, group_hbm, cluster_hbm, order_hbm, out_ref, emb_ref, ids, fetched,
           send, keys, msend, meta, kmeta, res, back, s1, r1, sm, rm, sy, ry, sc, rc, sd, rd, smx, rmx, sb, rb):
    points, width = emb_ref.shape
    cap = 2 * points // groups
    slots = groups * cap
    per = LANES // cap
    tiles = slots // LANES
    me = lax.axis_index("dp")
    own = lax.axis_index("blk")
    across = {"blk": flip(own, 2)}
    beside = {"blk": flip(own, 1)}
    partner = [None] + [{"dp": flip(me, k)} for k in perm[1:]]

    fetches = [
        pltpu.make_async_copy(group_hbm, ids.at[0], fetched.at[0]),
        pltpu.make_async_copy(cluster_hbm, ids.at[1], fetched.at[1]),
        pltpu.make_async_copy(order_hbm, ids.at[2], fetched.at[2]),
        pltpu.make_async_copy(emb_hbm, emb_ref, fetched.at[3]),
    ]
    for fetch in fetches:
        fetch.start()

    barrier = pltpu.get_barrier_semaphore()
    for who in partner[1:] + [across, beside]:
        pl.semaphore_signal(barrier, inc=1, device_id=who, device_id_type=MESH)

    def remote(src, dst, ssem, rsem, who):
        return pltpu.make_async_remote_copy(
            src_ref=src, dst_ref=dst, send_sem=ssem, recv_sem=rsem, device_id=who, device_id_type=MESH
        )

    for fetch in fetches[:3]:
        fetch.wait()
    group = ids[0]
    combined = ids[1] * total + ids[2] + 1
    flipped = jnp.bitwise_xor(group, me)
    relative = jnp.zeros_like(flipped)
    for i, k in enumerate(perm):
        relative = jnp.where(flipped == k, i, relative)
    member = lax.broadcasted_iota(jnp.int32, (groups, points), 0) == relative
    member_f = jnp.where(member, 1.0, 0.0)
    earlier = lax.broadcasted_iota(jnp.int32, (points, points), 0) < lax.broadcasted_iota(
        jnp.int32, (points, points), 1
    )
    before = jnp.dot(
        member_f.astype(jnp.bfloat16),
        jnp.where(earlier, 1.0, 0.0).astype(jnp.bfloat16),
        preferred_element_type=jnp.float32,
    )
    rank = jnp.sum(before * member_f, axis=0, keepdims=True).astype(jnp.int32)
    target = relative * cap + rank

    digits = jnp.concatenate(
        [combined & 127, (combined >> 7) & 127, combined >> 14, jnp.zeros((5, points), jnp.int32)], axis=0
    ).astype(jnp.float32).astype(jnp.bfloat16)
    lane_slot = lax.broadcasted_iota(jnp.int32, (LANES, points), 0) & (cap - 1)
    local_target = target & (cap - 1)
    same_rank = lane_slot == local_target
    for k in range(groups):
        pick = jnp.where(same_rank & (relative == k), 1.0, 0.0).astype(jnp.bfloat16)
        got = lax.dot_general(digits, pick, NT, preferred_element_type=jnp.float32)
        row = got[0:1, :] + 128.0 * got[1:2, :] + 16384.0 * got[2:3, :]
        row = jnp.broadcast_to(row.astype(jnp.int32), (8, LANES))
        if k == 0:
            meta[0, 0] = row
        else:
            msend[k] = row

    fetches[3].wait()
    values = emb_ref[...].astype(jnp.float32)
    scale = lax.rsqrt(jnp.mean(values * values, axis=1, keepdims=True) + 1e-06)
    unit = (values * scale * width ** (-0.5)).astype(jnp.bfloat16)

    pl.semaphore_wait(barrier, groups + 1)

    meta_copies = [None] * groups
    for i in range(1, groups):
        meta_copies[i] = remote(msend.at[i], meta.at[0, i], sm.at[i], rm.at[i], partner[i])
        meta_copies[i].start()

    first = [None] * groups
    over_y = [None] * groups
    over_c = [None] * groups
    diag = [None] * groups

    def forward(i):
        over_y[i] = remote(keys.at[0, i], keys.at[2, i], sy.at[i], ry.at[i], across)
        over_y[i].start()
        over_c[i] = remote(keys.at[0, i], keys.at[1, i], sc.at[i], rc.at[i], beside)
        over_c[i].start()

    def onward(i):
        over_y[i].wait_recv()
        diag[i] = remote(keys.at[2, i], keys.at[3, i], sd.at[i], rd.at[i], beside)
        diag[i].start()

    held_back = [i for i in range(1, groups) if i not in first_sends]
    slot_rows = lax.broadcasted_iota(jnp.int32, (cap, points), 0)
    for i in first_sends + held_back:
        place = jnp.where(slot_rows + i * cap == target, 1.0, 0.0).astype(jnp.bfloat16)
        rows = jnp.dot(place, unit, preferred_element_type=jnp.float32).astype(jnp.bfloat16)
        if i == 0:
            keys[0, 0] = rows
            forward(0)
        else:
            send[i] = rows
            first[i] = remote(send.at[i], keys.at[0, i], s1.at[i], r1.at[i], partner[i])
            if i not in held_back:
                first[i].start()

    def key_tiles(r):
        lane_block = lax.broadcasted_iota(jnp.int32, (1, LANES), 1) // cap
        rows = []
        for t in range(tiles):
            row = meta[r, t * per][0:1, :]
            for j in range(1, per):
                row = jnp.where(lane_block == j, meta[r, t * per + j][0:1, :], row)
            rows.append(row)
            kmeta[r, t] = jnp.broadcast_to(row, (LANES, LANES)).T
        return rows

    for i in range(1, groups):
        meta_copies[i].wait_recv()
    meta_y = remote(meta.at[0], meta.at[2], smx.at[0], rmx.at[0], across)
    meta_y.start()
    meta_c = remote(meta.at[0], meta.at[1], smx.at[1], rmx.at[1], beside)
    meta_c.start()
    query = key_tiles(0)
    floor = [(row - 1) & (-total) for row in query]
    best = [jnp.full((8, LANES), -2.0, jnp.float32) for _ in range(tiles)]

    def visit(r, t0, t1, q0, q1):
        block = keys[r, t0 * per:t1 * per].reshape((t1 - t0) * LANES, width)
        queries = keys[0, q0 * per:q1 * per].reshape((q1 - q0) * LANES, width)
        scores = lax.dot_general(block, queries, NT, preferred_element_type=jnp.float32)
        for t in range(t0, t1):
            mine = kmeta[r, t]
            for q in range(q0, q1):
                part = scores[(t - t0) * LANES:(t - t0 + 1) * LANES, (q - q0) * LANES:(q - q0 + 1) * LANES]
                part = jnp.where((mine < query[q]) & (mine > floor[q]), part, -2.0)
                best[q] = jnp.maximum(best[q], jnp.max(part.reshape(LANES // 8, 8, LANES), axis=0))

    def landed(r, t):
        for i in range(t * per, (t + 1) * per):
            if r == 1:
                over_c[i].wait_recv()
            if r == 3:
                diag[i].wait_recv()

    for i in range(1, groups):
        first[i].wait_recv()
        if perm[i] >= groups // 2 and held_back:
            first[held_back.pop(0)].start()
        forward(i)
        onward(i - 1)
        if i == 1:
            meta_c.wait_recv()
            key_tiles(1)
            meta_y.wait_recv()
            meta_d = remote(meta.at[2], meta.at[3], smx.at[2], rmx.at[2], beside)
            meta_d.start()
            key_tiles(2)
            meta_d.wait_recv()
            key_tiles(3)
        if i % per == 0:
            t = i // per - 1
            if t:
                for r in range(4):
                    visit(r, 0, t, t, t + 1)
            for r in (0, 2, 1, 3):
                landed(r, t)
                visit(r, t, t + 1, 0, t + 1)
    last = tiles - 1
    for r in range(4):
        visit(r, 0, last, last, tiles)
    visit(0, last, tiles, 0, tiles)
    landed(1, last)
    visit(1, last, tiles, 0, tiles)
    onward(groups - 1)
    visit(2, last, tiles, 0, tiles)
    landed(3, last)
    visit(3, last, tiles, 0, tiles)

    best = jnp.concatenate([jnp.max(part, axis=0, keepdims=True) for part in best], axis=1)
    answer = jnp.broadcast_to(jnp.where(best > -1.5, best, -1.0), (8, slots))
    for t in range(tiles):
        res[t] = answer[:, t * LANES:(t + 1) * LANES]
    back[0] = res[0]
    replies = [None] * groups
    for k in range(1, groups):
        replies[k] = remote(res.at[k // per], back.at[k], sb.at[k], rb.at[k], partner[k])
        replies[k].start()

    for k in range(groups):
        over_y[k].wait_send()
        over_c[k].wait_send()
        diag[k].wait_send()
        if k:
            first[k].wait_send()
            meta_copies[k].wait_send()
    meta_y.wait_send()
    meta_c.wait_send()
    meta_d.wait_send()

    lane_block = lax.broadcasted_iota(jnp.int32, (1, LANES), 1) // cap
    nearest = jnp.full((1, points), -2.0, jnp.float32)
    slot_iota = lax.broadcasted_iota(jnp.int32, (LANES, points), 0)
    for t in range(tiles):
        for j in range(per):
            if t * per + j:
                replies[t * per + j].wait_recv()
        row = back[t * per][0:1, :]
        for j in range(1, per):
            row = jnp.where(lane_block == j, back[t * per + j][0:1, :], row)
        column = jnp.broadcast_to(row, (LANES, LANES)).T
        column = jnp.concatenate([column] * (points // LANES), axis=1)
        hit = jnp.where(slot_iota + t * LANES == target, column, -2.0)
        nearest = jnp.maximum(nearest, jnp.max(hit, axis=0, keepdims=True))
    out_ref[...] = nearest.reshape(points)
    for k in range(1, groups):
        replies[k].wait_send()


def body(total, embeddings, point_group, point_cluster, point_order):
    groups = lax.axis_size("dp")
    blocks = lax.axis_size("blk")
    points, width = embeddings.shape
    cap = 2 * points // groups
    slots = groups * cap
    near, far = list(range(1, groups // 2)), list(range(groups // 2, groups))
    perm = [0, near[0]] + [k for pair in zip(near[1:], far) for k in pair] + far[len(near) - 1:]
    held = far[groups // 4:]
    first_sends = [k for k in [far[0], 0] + perm[1:] if k not in held]
    first_sends = [perm.index(k) for k in dict.fromkeys(first_sends)]
    dma = pltpu.SemaphoreType.DMA
    out = pl.pallas_call(
        functools.partial(kernel, groups, total, perm, first_sends),
        out_shape=jax.ShapeDtypeStruct((points,), jnp.float32),
        in_specs=[pl.BlockSpec(memory_space=pl.ANY)] * 4,
        out_specs=pl.BlockSpec(memory_space=pltpu.VMEM),
        scratch_shapes=[
            pltpu.VMEM((points, width), jnp.bfloat16),
            pltpu.VMEM((3, 1, points), jnp.int32),
            dma((4,)),
            pltpu.VMEM((groups, cap, width), jnp.bfloat16),
            pltpu.VMEM((blocks, groups, cap, width), jnp.bfloat16),
            pltpu.VMEM((groups, 8, LANES), jnp.int32),
            pltpu.VMEM((blocks, groups, 8, LANES), jnp.int32),
            pltpu.VMEM((blocks, slots // LANES, LANES, LANES), jnp.int32),
            pltpu.VMEM((slots // LANES, 8, LANES), jnp.float32),
            pltpu.VMEM((groups, 8, LANES), jnp.float32),
        ]
        + [dma((groups,))] * 10
        + [dma((3,))] * 2
        + [dma((groups,))] * 2,
        compiler_params=pltpu.CompilerParams(
            collective_id=0, has_side_effects=True, vmem_limit_bytes=64 * 1024 * 1024 - 65536
        ),
        cost_estimate=pl.CostEstimate(
            flops=2 * slots * slots * blocks * width, bytes_accessed=points * width * 2, transcendentals=points
        ),
    )(embeddings, point_group.reshape(1, points), point_cluster.reshape(1, points), point_order.reshape(1, points))
    return out


def solution(mesh):
    in_specs = (P(("dp", "blk"), None), P(("dp", "blk"), None), P(("dp", "blk")), P(("dp", "blk")))
    out_specs = P(("dp", "blk"))

    def run(embeddings, point_group, point_cluster, point_order):
        inner = functools.partial(body, embeddings.shape[0])
        return jax.shard_map(inner, mesh=mesh, in_specs=in_specs, out_specs=out_specs, check_vma=False)(
            embeddings, point_group, point_cluster, point_order
        )

    return run
```

```python
import functools

import jax
import jax.numpy as jnp
from jax import lax
from jax.experimental import pallas as pl
from jax.experimental.pallas import tpu as pltpu
from jax.sharding import PartitionSpec as P

CLG = 32
LANES = 128
MESH = pl.DeviceIdType.MESH
NT = (((1,), (1,)), ((), ()))


def flip(index, mask):
    out = index
    bit = 1
    while bit <= mask:
        if mask & bit:
            digit = lax.rem(lax.div(index, jnp.int32(bit)), jnp.int32(2))
            out = out + bit * (1 - 2 * digit)
        bit *= 2
    return out


def kernel(groups, total, perm, first_sends, emb_hbm, group_hbm, cluster_hbm, order_hbm, out_ref, emb_ref, ids, fetched,
           send, keys, msend, meta, kmeta, res, back, s1, r1, sm, rm, sy, ry, sc, rc, sd, rd, smx, rmx, sb, rb):
    points, width = emb_ref.shape
    cap = 2 * points // groups
    slots = groups * cap
    per = LANES // cap
    tiles = slots // LANES
    me = lax.axis_index("dp")
    own = lax.axis_index("blk")
    across = {"blk": flip(own, 2)}
    beside = {"blk": flip(own, 1)}
    partner = [None] + [{"dp": flip(me, k)} for k in perm[1:]]

    fetches = [
        pltpu.make_async_copy(group_hbm, ids.at[0], fetched.at[0]),
        pltpu.make_async_copy(cluster_hbm, ids.at[1], fetched.at[1]),
        pltpu.make_async_copy(order_hbm, ids.at[2], fetched.at[2]),
        pltpu.make_async_copy(emb_hbm, emb_ref, fetched.at[3]),
    ]
    for fetch in fetches:
        fetch.start()

    barrier = pltpu.get_barrier_semaphore()
    for who in partner[1:] + [across, beside]:
        pl.semaphore_signal(barrier, inc=1, device_id=who, device_id_type=MESH)

    def remote(src, dst, ssem, rsem, who):
        return pltpu.make_async_remote_copy(
            src_ref=src, dst_ref=dst, send_sem=ssem, recv_sem=rsem, device_id=who, device_id_type=MESH
        )

    for fetch in fetches[:3]:
        fetch.wait()
    group = ids[0]
    combined = ids[1] * total + ids[2] + 1
    flipped = jnp.bitwise_xor(group, me)
    relative = jnp.zeros_like(flipped)
    for i, k in enumerate(perm):
        relative = jnp.where(flipped == k, i, relative)
    member = lax.broadcasted_iota(jnp.int32, (groups, points), 0) == relative
    member_f = jnp.where(member, 1.0, 0.0)
    earlier = lax.broadcasted_iota(jnp.int32, (points, points), 0) < lax.broadcasted_iota(
        jnp.int32, (points, points), 1
    )
    before = jnp.dot(
        member_f.astype(jnp.bfloat16),
        jnp.where(earlier, 1.0, 0.0).astype(jnp.bfloat16),
        preferred_element_type=jnp.float32,
    )
    rank = jnp.sum(before * member_f, axis=0, keepdims=True).astype(jnp.int32)
    target = relative * cap + rank

    digits = jnp.concatenate(
        [combined & 127, (combined >> 7) & 127, combined >> 14, jnp.zeros((5, points), jnp.int32)], axis=0
    ).astype(jnp.float32).astype(jnp.bfloat16)
    lane_slot = lax.broadcasted_iota(jnp.int32, (LANES, points), 0) & (cap - 1)
    local_target = target & (cap - 1)
    same_rank = lane_slot == local_target
    for k in range(groups):
        pick = jnp.where(same_rank & (relative == k), 1.0, 0.0).astype(jnp.bfloat16)
        got = lax.dot_general(digits, pick, NT, preferred_element_type=jnp.float32)
        row = got[0:1, :] + 128.0 * got[1:2, :] + 16384.0 * got[2:3, :]
        row = jnp.broadcast_to(row.astype(jnp.int32), (8, LANES))
        if k == 0:
            meta[0, 0] = row
        else:
            msend[k] = row

    fetches[3].wait()
    values = emb_ref[...].astype(jnp.float32)
    scale = lax.rsqrt(jnp.mean(values * values, axis=1, keepdims=True) + 1e-06)
    unit = (values * scale * width ** (-0.5)).astype(jnp.bfloat16)

    pl.semaphore_wait(barrier, groups + 1)

    meta_copies = [None] * groups
    for i in range(1, groups):
        meta_copies[i] = remote(msend.at[i], meta.at[0, i], sm.at[i], rm.at[i], partner[i])
        meta_copies[i].start()

    first = [None] * groups
    over_y = [None] * groups
    over_c = [None] * groups
    diag = [None] * groups

    def forward(i):
        over_y[i] = remote(keys.at[0, i], keys.at[2, i], sy.at[i], ry.at[i], across)
        over_y[i].start()
        over_c[i] = remote(keys.at[0, i], keys.at[1, i], sc.at[i], rc.at[i], beside)
        over_c[i].start()

    def onward(i):
        over_y[i].wait_recv()
        diag[i] = remote(keys.at[2, i], keys.at[3, i], sd.at[i], rd.at[i], beside)
        diag[i].start()

    held_back = [i for i in range(1, groups) if i not in first_sends]
    slot_rows = lax.broadcasted_iota(jnp.int32, (cap, points), 0)
    for i in first_sends + held_back:
        place = jnp.where(slot_rows + i * cap == target, 1.0, 0.0).astype(jnp.bfloat16)
        rows = jnp.dot(place, unit, preferred_element_type=jnp.float32).astype(jnp.bfloat16)
        if i == 0:
            keys[0, 0] = rows
            forward(0)
        else:
            send[i] = rows
            first[i] = remote(send.at[i], keys.at[0, i], s1.at[i], r1.at[i], partner[i])
            if i not in held_back:
                first[i].start()

    def key_tiles(r):
        lane_block = lax.broadcasted_iota(jnp.int32, (1, LANES), 1) // cap
        rows = []
        for t in range(tiles):
            row = meta[r, t * per][0:1, :]
            for j in range(1, per):
                row = jnp.where(lane_block == j, meta[r, t * per + j][0:1, :], row)
            rows.append(row)
            kmeta[r, t] = jnp.broadcast_to(row, (LANES, LANES)).T
        return rows

    for i in range(1, groups):
        meta_copies[i].wait_recv()
    meta_y = remote(meta.at[0], meta.at[2], smx.at[0], rmx.at[0], across)
    meta_y.start()
    meta_c = remote(meta.at[0], meta.at[1], smx.at[1], rmx.at[1], beside)
    meta_c.start()
    query = key_tiles(0)
    floor = [(row - 1) & (-total) for row in query]
    best = [jnp.full((8, LANES), -2.0, jnp.float32) for _ in range(tiles)]

    def visit(r, t0, t1, q0, q1):
        block = keys[r, t0 * per:t1 * per].reshape((t1 - t0) * LANES, width)
        queries = keys[0, q0 * per:q1 * per].reshape((q1 - q0) * LANES, width)
        scores = lax.dot_general(block, queries, NT, preferred_element_type=jnp.float32)
        for t in range(t0, t1):
            mine = kmeta[r, t]
            for q in range(q0, q1):
                part = scores[(t - t0) * LANES:(t - t0 + 1) * LANES, (q - q0) * LANES:(q - q0 + 1) * LANES]
                part = jnp.where((mine < query[q]) & (mine > floor[q]), part, -2.0)
                best[q] = jnp.maximum(best[q], jnp.max(part.reshape(LANES // 8, 8, LANES), axis=0))

    def landed(r, t):
        for i in range(t * per, (t + 1) * per):
            if r == 1:
                over_c[i].wait_recv()
            if r == 3:
                diag[i].wait_recv()

    for i in range(1, groups):
        first[i].wait_recv()
        if held_back:
            first[held_back.pop(0)].start()
        forward(i)
        onward(i - 1)
        if i == 1:
            meta_y.wait_recv()
            meta_d = remote(meta.at[2], meta.at[3], smx.at[2], rmx.at[2], beside)
            meta_d.start()
        if i == per:
            meta_c.wait_recv()
            key_tiles(1)
            key_tiles(2)
            meta_d.wait_recv()
            key_tiles(3)
        if i % per == 0:
            t = i // per - 1
            if t:
                for r in range(4):
                    visit(r, 0, t, t, t + 1)
            for r in (0, 2, 1, 3):
                landed(r, t)
                visit(r, t, t + 1, 0, t + 1)
    last = tiles - 1
    for r in range(4):
        visit(r, 0, last, last, tiles)
    visit(0, last, tiles, 0, tiles)
    landed(1, last)
    visit(1, last, tiles, 0, tiles)
    onward(groups - 1)
    visit(2, last, tiles, 0, tiles)
    landed(3, last)
    visit(3, last, tiles, 0, tiles)

    best = jnp.concatenate([jnp.max(part, axis=0, keepdims=True) for part in best], axis=1)
    answer = jnp.broadcast_to(jnp.where(best > -1.5, best, -1.0), (8, slots))
    for t in range(tiles):
        res[t] = answer[:, t * LANES:(t + 1) * LANES]
    back[0] = res[0]
    replies = [None] * groups
    for k in range(1, groups):
        replies[k] = remote(res.at[k // per], back.at[k], sb.at[k], rb.at[k], partner[k])
        replies[k].start()

    for k in range(groups):
        over_y[k].wait_send()
        over_c[k].wait_send()
        diag[k].wait_send()
        if k:
            first[k].wait_send()
            meta_copies[k].wait_send()
    meta_y.wait_send()
    meta_c.wait_send()
    meta_d.wait_send()

    lane_block = lax.broadcasted_iota(jnp.int32, (1, LANES), 1) // cap
    nearest = jnp.full((1, points), -2.0, jnp.float32)
    slot_iota = lax.broadcasted_iota(jnp.int32, (LANES, points), 0)
    for t in range(tiles):
        for j in range(per):
            if t * per + j:
                replies[t * per + j].wait_recv()
        row = back[t * per][0:1, :]
        for j in range(1, per):
            row = jnp.where(lane_block == j, back[t * per + j][0:1, :], row)
        column = jnp.broadcast_to(row, (LANES, LANES)).T
        column = jnp.concatenate([column] * (points // LANES), axis=1)
        hit = jnp.where(slot_iota + t * LANES == target, column, -2.0)
        nearest = jnp.maximum(nearest, jnp.max(hit, axis=0, keepdims=True))
    out_ref[...] = nearest.reshape(points)
    for k in range(1, groups):
        replies[k].wait_send()


def body(total, embeddings, point_group, point_cluster, point_order):
    groups = lax.axis_size("dp")
    blocks = lax.axis_size("blk")
    points, width = embeddings.shape
    cap = 2 * points // groups
    slots = groups * cap
    near, far = list(range(1, groups // 2)), list(range(groups // 2, groups))
    perm = [0] + [k for pair in zip(near, far) for k in pair] + far[len(near):]
    first_sends = [2, 0, 1]
    dma = pltpu.SemaphoreType.DMA
    out = pl.pallas_call(
        functools.partial(kernel, groups, total, perm, first_sends),
        out_shape=jax.ShapeDtypeStruct((points,), jnp.float32),
        in_specs=[pl.BlockSpec(memory_space=pl.ANY)] * 4,
        out_specs=pl.BlockSpec(memory_space=pltpu.VMEM),
        scratch_shapes=[
            pltpu.VMEM((points, width), jnp.bfloat16),
            pltpu.VMEM((3, 1, points), jnp.int32),
            dma((4,)),
            pltpu.VMEM((groups, cap, width), jnp.bfloat16),
            pltpu.VMEM((blocks, groups, cap, width), jnp.bfloat16),
            pltpu.VMEM((groups, 8, LANES), jnp.int32),
            pltpu.VMEM((blocks, groups, 8, LANES), jnp.int32),
            pltpu.VMEM((blocks, slots // LANES, LANES, LANES), jnp.int32),
            pltpu.VMEM((slots // LANES, 8, LANES), jnp.float32),
            pltpu.VMEM((groups, 8, LANES), jnp.float32),
        ]
        + [dma((groups,))] * 10
        + [dma((3,))] * 2
        + [dma((groups,))] * 2,
        compiler_params=pltpu.CompilerParams(
            collective_id=0, has_side_effects=True, vmem_limit_bytes=64 * 1024 * 1024 - 65536
        ),
        cost_estimate=pl.CostEstimate(
            flops=2 * slots * slots * blocks * width, bytes_accessed=points * width * 2, transcendentals=points
        ),
    )(embeddings, point_group.reshape(1, points), point_cluster.reshape(1, points), point_order.reshape(1, points))
    return out


def solution(mesh):
    in_specs = (P(("dp", "blk"), None), P(("dp", "blk"), None), P(("dp", "blk")), P(("dp", "blk")))
    out_specs = P(("dp", "blk"))

    def run(embeddings, point_group, point_cluster, point_order):
        inner = functools.partial(body, embeddings.shape[0])
        return jax.shard_map(inner, mesh=mesh, in_specs=in_specs, out_specs=out_specs, check_vma=False)(
            embeddings, point_group, point_cluster, point_order
        )

    return run
```

```python
import functools

import jax
import jax.numpy as jnp
from jax import lax
from jax.experimental import pallas as pl
from jax.experimental.pallas import tpu as pltpu
from jax.sharding import PartitionSpec as P

CLG = 32
LANES = 128
MESH = pl.DeviceIdType.MESH
NT = (((1,), (1,)), ((), ()))


def flip(index, mask):
    out = index
    bit = 1
    while bit <= mask:
        if mask & bit:
            digit = lax.rem(lax.div(index, jnp.int32(bit)), jnp.int32(2))
            out = out + bit * (1 - 2 * digit)
        bit *= 2
    return out


def kernel(groups, total, perm, first_sends, emb_hbm, group_hbm, cluster_hbm, order_hbm, out_ref, emb_ref, ids, fetched,
           send, keys, msend, meta, kmeta, res, back, s1, r1, sm, rm, sy, ry, sc, rc, sd, rd, smx, rmx, sb, rb):
    points, width = emb_ref.shape
    cap = 2 * points // groups
    slots = groups * cap
    per = LANES // cap
    tiles = slots // LANES
    me = lax.axis_index("dp")
    own = lax.axis_index("blk")
    across = {"blk": flip(own, 2)}
    beside = {"blk": flip(own, 1)}
    partner = [None] + [{"dp": flip(me, k)} for k in perm[1:]]

    fetches = [
        pltpu.make_async_copy(group_hbm, ids.at[0], fetched.at[0]),
        pltpu.make_async_copy(cluster_hbm, ids.at[1], fetched.at[1]),
        pltpu.make_async_copy(order_hbm, ids.at[2], fetched.at[2]),
        pltpu.make_async_copy(emb_hbm, emb_ref, fetched.at[3]),
    ]
    for fetch in fetches:
        fetch.start()

    barrier = pltpu.get_barrier_semaphore()
    for who in partner[1:] + [across, beside]:
        pl.semaphore_signal(barrier, inc=1, device_id=who, device_id_type=MESH)

    def remote(src, dst, ssem, rsem, who):
        return pltpu.make_async_remote_copy(
            src_ref=src, dst_ref=dst, send_sem=ssem, recv_sem=rsem, device_id=who, device_id_type=MESH
        )

    for fetch in fetches[:3]:
        fetch.wait()
    group = ids[0]
    combined = ids[1] * total + ids[2] + 1
    flipped = jnp.bitwise_xor(group, me)
    relative = jnp.zeros_like(flipped)
    for i, k in enumerate(perm):
        relative = jnp.where(flipped == k, i, relative)
    member = lax.broadcasted_iota(jnp.int32, (groups, points), 0) == relative
    member_f = jnp.where(member, 1.0, 0.0)
    earlier = lax.broadcasted_iota(jnp.int32, (points, points), 0) < lax.broadcasted_iota(
        jnp.int32, (points, points), 1
    )
    before = jnp.dot(
        member_f.astype(jnp.bfloat16),
        jnp.where(earlier, 1.0, 0.0).astype(jnp.bfloat16),
        preferred_element_type=jnp.float32,
    )
    rank = jnp.sum(before * member_f, axis=0, keepdims=True).astype(jnp.int32)
    target = relative * cap + rank

    fetches[3].wait()
    values = emb_ref[...].astype(jnp.float32)
    scale = lax.rsqrt(jnp.mean(values * values, axis=1, keepdims=True) + 1e-06)
    unit = (values * scale * width ** (-0.5)).astype(jnp.bfloat16)

    slot_rows = lax.broadcasted_iota(jnp.int32, (cap, points), 0)

    def slotted(i):
        place = jnp.where(slot_rows + i * cap == target, 1.0, 0.0).astype(jnp.bfloat16)
        return jnp.dot(place, unit, preferred_element_type=jnp.float32).astype(jnp.bfloat16)

    for i in first_sends:
        if i == 0:
            keys[0, 0] = slotted(0)
        else:
            send[i] = slotted(i)

    pl.semaphore_wait(barrier, groups + 1)

    first = [None] * groups
    over_y = [None] * groups
    over_c = [None] * groups
    diag = [None] * groups

    def forward(i):
        over_y[i] = remote(keys.at[0, i], keys.at[2, i], sy.at[i], ry.at[i], across)
        over_y[i].start()
        over_c[i] = remote(keys.at[0, i], keys.at[1, i], sc.at[i], rc.at[i], beside)
        over_c[i].start()

    def onward(i):
        over_y[i].wait_recv()
        diag[i] = remote(keys.at[2, i], keys.at[3, i], sd.at[i], rd.at[i], beside)
        diag[i].start()

    def emit(i):
        first[i] = remote(send.at[i], keys.at[0, i], s1.at[i], r1.at[i], partner[i])
        first[i].start()

    for i in first_sends:
        if i == 0:
            forward(0)
        else:
            emit(i)
    held_back = [i for i in range(1, groups) if i not in first_sends]
    digits = jnp.concatenate(
        [combined & 127, (combined >> 7) & 127, combined >> 14, jnp.zeros((5, points), jnp.int32)], axis=0
    ).astype(jnp.float32).astype(jnp.bfloat16)
    lane_slot = lax.broadcasted_iota(jnp.int32, (LANES, points), 0) & (cap - 1)
    local_target = target & (cap - 1)
    same_rank = lane_slot == local_target
    for k in range(groups):
        pick = jnp.where(same_rank & (relative == k), 1.0, 0.0).astype(jnp.bfloat16)
        got = lax.dot_general(digits, pick, NT, preferred_element_type=jnp.float32)
        row = got[0:1, :] + 128.0 * got[1:2, :] + 16384.0 * got[2:3, :]
        row = jnp.broadcast_to(row.astype(jnp.int32), (8, LANES))
        if k == 0:
            meta[0, 0] = row
        else:
            msend[k] = row

    meta_copies = [None] * groups
    for i in range(1, groups):
        meta_copies[i] = remote(msend.at[i], meta.at[0, i], sm.at[i], rm.at[i], partner[i])
        meta_copies[i].start()

    for i in held_back:
        send[i] = slotted(i)

    def key_tiles(r):
        lane_block = lax.broadcasted_iota(jnp.int32, (1, LANES), 1) // cap
        rows = []
        for t in range(tiles):
            row = meta[r, t * per][0:1, :]
            for j in range(1, per):
                row = jnp.where(lane_block == j, meta[r, t * per + j][0:1, :], row)
            rows.append(row)
            kmeta[r, t] = jnp.broadcast_to(row, (LANES, LANES)).T
        return rows

    for i in range(1, groups):
        meta_copies[i].wait_recv()
    meta_y = remote(meta.at[0], meta.at[2], smx.at[0], rmx.at[0], across)
    meta_y.start()
    meta_c = remote(meta.at[0], meta.at[1], smx.at[1], rmx.at[1], beside)
    meta_c.start()
    ready, scored = False, 0
    best = [jnp.full((8, LANES), -2.0, jnp.float32) for _ in range(tiles)]

    def visit(r, t0, t1, q0, q1):
        block = keys[r, t0 * per:t1 * per].reshape((t1 - t0) * LANES, width)
        queries = keys[0, q0 * per:q1 * per].reshape((q1 - q0) * LANES, width)
        scores = lax.dot_general(block, queries, NT, preferred_element_type=jnp.float32)
        for t in range(t0, t1):
            mine = kmeta[r, t]
            for q in range(q0, q1):
                part = scores[(t - t0) * LANES:(t - t0 + 1) * LANES, (q - q0) * LANES:(q - q0 + 1) * LANES]
                part = jnp.where((mine < query[q]) & (mine > floor[q]), part, -2.0)
                best[q] = jnp.maximum(best[q], jnp.max(part.reshape(LANES // 8, 8, LANES), axis=0))

    def landed(r, t):
        for i in range(t * per, (t + 1) * per):
            if r == 1:
                over_c[i].wait_recv()
            if r == 3:
                diag[i].wait_recv()

    for i in range(1, groups):
        first[i].wait_recv()
        if (i == 1 or perm[i] >= groups // 2) and held_back:
            emit(held_back.pop(0))
        forward(i)
        onward(i - 1)
        if i == 1:
            meta_y.wait_recv()
            meta_d = remote(meta.at[2], meta.at[3], smx.at[2], rmx.at[2], beside)
            meta_d.start()
        if held_back or i == groups - 1:
            continue
        if not ready:
            meta_c.wait_recv()
            meta_d.wait_recv()
            query = key_tiles(0)
            floor = [(row - 1) & (-total) for row in query]
            for r in (1, 2, 3):
                key_tiles(r)
            ready = True
        while scored < i // per:
            t = scored
            scored += 1
            if t:
                for r in range(4):
                    visit(r, 0, t, t, t + 1)
            for r in (0, 2, 1, 3):
                landed(r, t)
                visit(r, t, t + 1, 0, t + 1)
    last = tiles - 1
    assert ready and scored == last
    for r in range(4):
        visit(r, 0, last, last, tiles)
    visit(0, last, tiles, 0, tiles)
    landed(1, last)
    visit(1, last, tiles, 0, tiles)
    onward(groups - 1)
    visit(2, last, tiles, 0, tiles)
    landed(3, last)
    visit(3, last, tiles, 0, tiles)

    best = jnp.concatenate([jnp.max(part, axis=0, keepdims=True) for part in best], axis=1)
    answer = jnp.broadcast_to(jnp.where(best > -1.5, best, -1.0), (8, slots))
    for t in range(tiles):
        res[t] = answer[:, t * LANES:(t + 1) * LANES]
    back[0] = res[0]
    replies = [None] * groups
    for k in range(1, groups):
        replies[k] = remote(res.at[k // per], back.at[k], sb.at[k], rb.at[k], partner[k])
        replies[k].start()

    for k in range(groups):
        over_y[k].wait_send()
        over_c[k].wait_send()
        diag[k].wait_send()
        if k:
            first[k].wait_send()
            meta_copies[k].wait_send()
    meta_y.wait_send()
    meta_c.wait_send()
    meta_d.wait_send()

    lane_block = lax.broadcasted_iota(jnp.int32, (1, LANES), 1) // cap
    nearest = jnp.full((1, points), -2.0, jnp.float32)
    slot_iota = lax.broadcasted_iota(jnp.int32, (LANES, points), 0)
    for t in range(tiles):
        for j in range(per):
            if t * per + j:
                replies[t * per + j].wait_recv()
        row = back[t * per][0:1, :]
        for j in range(1, per):
            row = jnp.where(lane_block == j, back[t * per + j][0:1, :], row)
        column = jnp.broadcast_to(row, (LANES, LANES)).T
        column = jnp.concatenate([column] * (points // LANES), axis=1)
        hit = jnp.where(slot_iota + t * LANES == target, column, -2.0)
        nearest = jnp.maximum(nearest, jnp.max(hit, axis=0, keepdims=True))
    out_ref[...] = nearest.reshape(points)
    for k in range(1, groups):
        replies[k].wait_send()


def body(total, embeddings, point_group, point_cluster, point_order):
    groups = lax.axis_size("dp")
    blocks = lax.axis_size("blk")
    points, width = embeddings.shape
    cap = 2 * points // groups
    slots = groups * cap
    near, far = list(range(1, groups // 2)), list(range(groups // 2, groups))
    perm = [0, near[0]] + [k for pair in zip(near[1:], far) for k in pair] + far[len(near) - 1:]
    held = far[1:]
    first_sends = [perm.index(k) for k in [far[0], 0] + near]
    dma = pltpu.SemaphoreType.DMA
    out = pl.pallas_call(
        functools.partial(kernel, groups, total, perm, first_sends),
        out_shape=jax.ShapeDtypeStruct((points,), jnp.float32),
        in_specs=[pl.BlockSpec(memory_space=pl.ANY)] * 4,
        out_specs=pl.BlockSpec(memory_space=pltpu.VMEM),
        scratch_shapes=[
            pltpu.VMEM((points, width), jnp.bfloat16),
            pltpu.VMEM((3, 1, points), jnp.int32),
            dma((4,)),
            pltpu.VMEM((groups, cap, width), jnp.bfloat16),
            pltpu.VMEM((blocks, groups, cap, width), jnp.bfloat16),
            pltpu.VMEM((groups, 8, LANES), jnp.int32),
            pltpu.VMEM((blocks, groups, 8, LANES), jnp.int32),
            pltpu.VMEM((blocks, slots // LANES, LANES, LANES), jnp.int32),
            pltpu.VMEM((slots // LANES, 8, LANES), jnp.float32),
            pltpu.VMEM((groups, 8, LANES), jnp.float32),
        ]
        + [dma((groups,))] * 10
        + [dma((3,))] * 2
        + [dma((groups,))] * 2,
        compiler_params=pltpu.CompilerParams(
            collective_id=0, has_side_effects=True, vmem_limit_bytes=64 * 1024 * 1024 - 65536
        ),
        cost_estimate=pl.CostEstimate(
            flops=2 * slots * slots * blocks * width, bytes_accessed=points * width * 2, transcendentals=points
        ),
    )(embeddings, point_group.reshape(1, points), point_cluster.reshape(1, points), point_order.reshape(1, points))
    return out


def solution(mesh):
    in_specs = (P(("dp", "blk"), None), P(("dp", "blk"), None), P(("dp", "blk")), P(("dp", "blk")))
    out_specs = P(("dp", "blk"))

    def run(embeddings, point_group, point_cluster, point_order):
        inner = functools.partial(body, embeddings.shape[0])
        return jax.shard_map(inner, mesh=mesh, in_specs=in_specs, out_specs=out_specs, check_vma=False)(
            embeddings, point_group, point_cluster, point_order
        )

    return run
```

```python
import functools

import jax
import jax.numpy as jnp
from jax import lax
from jax.experimental import pallas as pl
from jax.experimental.pallas import tpu as pltpu
from jax.sharding import PartitionSpec as P

CLG = 32
LANES = 128
MESH = pl.DeviceIdType.MESH
NT = (((1,), (1,)), ((), ()))


def flip(index, mask):
    out = index
    bit = 1
    while bit <= mask:
        if mask & bit:
            digit = lax.rem(lax.div(index, jnp.int32(bit)), jnp.int32(2))
            out = out + bit * (1 - 2 * digit)
        bit *= 2
    return out


def kernel(groups, total, perm, first_sends, emb_hbm, group_hbm, cluster_hbm, order_hbm, out_ref, emb_ref, ids, fetched,
           send, keys, msend, meta, kmeta, res, back, s1, r1, sm, rm, sy, ry, sc, rc, sd, rd, smx, rmx, sb, rb):
    points, width = emb_ref.shape
    cap = 2 * points // groups
    slots = groups * cap
    per = LANES // cap
    tiles = slots // LANES
    me = lax.axis_index("dp")
    own = lax.axis_index("blk")
    across = {"blk": flip(own, 2)}
    beside = {"blk": flip(own, 1)}
    partner = [None] + [{"dp": flip(me, k)} for k in perm[1:]]

    fetches = [
        pltpu.make_async_copy(group_hbm, ids.at[0], fetched.at[0]),
        pltpu.make_async_copy(cluster_hbm, ids.at[1], fetched.at[1]),
        pltpu.make_async_copy(order_hbm, ids.at[2], fetched.at[2]),
        pltpu.make_async_copy(emb_hbm, emb_ref, fetched.at[3]),
    ]
    for fetch in fetches:
        fetch.start()

    barrier = pltpu.get_barrier_semaphore()
    for who in partner[1:] + [across, beside]:
        pl.semaphore_signal(barrier, inc=1, device_id=who, device_id_type=MESH)

    def remote(src, dst, ssem, rsem, who):
        return pltpu.make_async_remote_copy(
            src_ref=src, dst_ref=dst, send_sem=ssem, recv_sem=rsem, device_id=who, device_id_type=MESH
        )

    for fetch in fetches[:3]:
        fetch.wait()
    group = ids[0]
    combined = ids[1] * total + ids[2] + 1
    flipped = jnp.bitwise_xor(group, me)
    relative = jnp.zeros_like(flipped)
    for i, k in enumerate(perm):
        relative = jnp.where(flipped == k, i, relative)
    member = lax.broadcasted_iota(jnp.int32, (groups, points), 0) == relative
    member_f = jnp.where(member, 1.0, 0.0)
    earlier = lax.broadcasted_iota(jnp.int32, (points, points), 0) < lax.broadcasted_iota(
        jnp.int32, (points, points), 1
    )
    before = jnp.dot(
        member_f.astype(jnp.bfloat16),
        jnp.where(earlier, 1.0, 0.0).astype(jnp.bfloat16),
        preferred_element_type=jnp.float32,
    )
    rank = jnp.sum(before * member_f, axis=0, keepdims=True).astype(jnp.int32)
    target = relative * cap + rank

    fetches[3].wait()
    values = emb_ref[...].astype(jnp.float32)
    scale = lax.rsqrt(jnp.mean(values * values, axis=1, keepdims=True) + 1e-06)
    unit = (values * scale * width ** (-0.5)).astype(jnp.bfloat16)

    slot_rows = lax.broadcasted_iota(jnp.int32, (cap, points), 0)

    def slotted(i):
        place = jnp.where(slot_rows + i * cap == target, 1.0, 0.0).astype(jnp.bfloat16)
        return jnp.dot(place, unit, preferred_element_type=jnp.float32).astype(jnp.bfloat16)

    pl.semaphore_wait(barrier, groups + 1)

    first = [None] * groups
    over_y = [None] * groups
    over_c = [None] * groups
    diag = [None] * groups

    def forward(i):
        over_y[i] = remote(keys.at[0, i], keys.at[2, i], sy.at[i], ry.at[i], across)
        over_y[i].start()
        over_c[i] = remote(keys.at[0, i], keys.at[1, i], sc.at[i], rc.at[i], beside)
        over_c[i].start()

    def onward(i):
        over_y[i].wait_recv()
        diag[i] = remote(keys.at[2, i], keys.at[3, i], sd.at[i], rd.at[i], beside)
        diag[i].start()

    def emit(i):
        first[i] = remote(send.at[i], keys.at[0, i], s1.at[i], r1.at[i], partner[i])
        first[i].start()

    for i in first_sends:
        if i == 0:
            keys[0, 0] = slotted(0)
            forward(0)
        else:
            send[i] = slotted(i)
            emit(i)

    digits = jnp.concatenate(
        [combined & 127, (combined >> 7) & 127, combined >> 14, jnp.zeros((5, points), jnp.int32)], axis=0
    ).astype(jnp.float32).astype(jnp.bfloat16)
    lane_slot = lax.broadcasted_iota(jnp.int32, (LANES, points), 0) & (cap - 1)
    local_target = target & (cap - 1)
    same_rank = lane_slot == local_target
    for k in range(groups):
        pick = jnp.where(same_rank & (relative == k), 1.0, 0.0).astype(jnp.bfloat16)
        got = lax.dot_general(digits, pick, NT, preferred_element_type=jnp.float32)
        row = got[0:1, :] + 128.0 * got[1:2, :] + 16384.0 * got[2:3, :]
        row = jnp.broadcast_to(row.astype(jnp.int32), (8, LANES))
        if k == 0:
            meta[0, 0] = row
        else:
            msend[k] = row

    meta_copies = [None] * groups
    for i in range(1, groups):
        meta_copies[i] = remote(msend.at[i], meta.at[0, i], sm.at[i], rm.at[i], partner[i])
        meta_copies[i].start()

    def key_tiles(r):
        lane_block = lax.broadcasted_iota(jnp.int32, (1, LANES), 1) // cap
        rows = []
        for t in range(tiles):
            row = meta[r, t * per][0:1, :]
            for j in range(1, per):
                row = jnp.where(lane_block == j, meta[r, t * per + j][0:1, :], row)
            rows.append(row)
            kmeta[r, t] = jnp.broadcast_to(row, (LANES, LANES)).T
        return rows

    for i in range(1, groups):
        meta_copies[i].wait_recv()
    meta_y = remote(meta.at[0], meta.at[2], smx.at[0], rmx.at[0], across)
    meta_y.start()
    meta_c = remote(meta.at[0], meta.at[1], smx.at[1], rmx.at[1], beside)
    meta_c.start()
    best = [jnp.full((8, LANES), -2.0, jnp.float32) for _ in range(tiles)]

    def visit(r, t0, t1, q0, q1):
        block = keys[r, t0 * per:t1 * per].reshape((t1 - t0) * LANES, width)
        queries = keys[0, q0 * per:q1 * per].reshape((q1 - q0) * LANES, width)
        scores = lax.dot_general(block, queries, NT, preferred_element_type=jnp.float32)
        for t in range(t0, t1):
            mine = kmeta[r, t]
            for q in range(q0, q1):
                part = scores[(t - t0) * LANES:(t - t0 + 1) * LANES, (q - q0) * LANES:(q - q0 + 1) * LANES]
                part = jnp.where((mine < query[q]) & (mine > floor[q]), part, -2.0)
                best[q] = jnp.maximum(best[q], jnp.max(part.reshape(LANES // 8, 8, LANES), axis=0))

    def landed(r, t0, t1):
        for i in range(t0 * per, t1 * per):
            if r == 1:
                over_c[i].wait_recv()
            if r == 3:
                diag[i].wait_recv()

    middle = groups // 2
    half = tiles // 2
    for i in range(1, middle):
        first[i].wait_recv()
        forward(i)
        onward(i - 1)
        if i == 1:
            meta_y.wait_recv()
            meta_d = remote(meta.at[2], meta.at[3], smx.at[2], rmx.at[2], beside)
            meta_d.start()
    onward(middle - 1)
    meta_c.wait_recv()
    meta_d.wait_recv()
    query = key_tiles(0)
    floor = [(row - 1) & (-total) for row in query]
    for r in (1, 2, 3):
        key_tiles(r)
    for r in range(4):
        landed(r, 0, half)
        visit(r, 0, half, 0, half)

    for i in range(middle, groups):
        first[i].wait_recv()
        forward(i)
    for r in range(4):
        visit(r, 0, half, half, tiles)
    visit(0, half, tiles, 0, tiles)
    for i in range(middle, groups):
        onward(i)
    landed(1, half, tiles)
    visit(1, half, tiles, 0, tiles)
    visit(2, half, tiles, 0, tiles)
    landed(3, half, tiles)
    visit(3, half, tiles, 0, tiles)

    best = jnp.concatenate([jnp.max(part, axis=0, keepdims=True) for part in best], axis=1)
    answer = jnp.broadcast_to(jnp.where(best > -1.5, best, -1.0), (8, slots))
    for t in range(tiles):
        res[t] = answer[:, t * LANES:(t + 1) * LANES]
    back[0] = res[0]
    replies = [None] * groups
    for k in range(1, groups):
        replies[k] = remote(res.at[k // per], back.at[k], sb.at[k], rb.at[k], partner[k])
        replies[k].start()

    for k in range(groups):
        over_y[k].wait_send()
        over_c[k].wait_send()
        diag[k].wait_send()
        if k:
            first[k].wait_send()
            meta_copies[k].wait_send()
    meta_y.wait_send()
    meta_c.wait_send()
    meta_d.wait_send()

    lane_block = lax.broadcasted_iota(jnp.int32, (1, LANES), 1) // cap
    nearest = jnp.full((1, points), -2.0, jnp.float32)
    slot_iota = lax.broadcasted_iota(jnp.int32, (LANES, points), 0)
    for t in range(tiles):
        for j in range(per):
            if t * per + j:
                replies[t * per + j].wait_recv()
        row = back[t * per][0:1, :]
        for j in range(1, per):
            row = jnp.where(lane_block == j, back[t * per + j][0:1, :], row)
        column = jnp.broadcast_to(row, (LANES, LANES)).T
        column = jnp.concatenate([column] * (points // LANES), axis=1)
        hit = jnp.where(slot_iota + t * LANES == target, column, -2.0)
        nearest = jnp.maximum(nearest, jnp.max(hit, axis=0, keepdims=True))
    out_ref[...] = nearest.reshape(points)
    for k in range(1, groups):
        replies[k].wait_send()


def body(total, embeddings, point_group, point_cluster, point_order):
    groups = lax.axis_size("dp")
    blocks = lax.axis_size("blk")
    points, width = embeddings.shape
    cap = 2 * points // groups
    slots = groups * cap
    near, far = list(range(1, groups // 2)), list(range(groups // 2, groups))
    perm = [0] + near + far
    first_sends = [near[0], 0] + [k for pair in zip(far, near[1:]) for k in pair] + far[len(near) - 1:]
    dma = pltpu.SemaphoreType.DMA
    out = pl.pallas_call(
        functools.partial(kernel, groups, total, perm, first_sends),
        out_shape=jax.ShapeDtypeStruct((points,), jnp.float32),
        in_specs=[pl.BlockSpec(memory_space=pl.ANY)] * 4,
        out_specs=pl.BlockSpec(memory_space=pltpu.VMEM),
        scratch_shapes=[
            pltpu.VMEM((points, width), jnp.bfloat16),
            pltpu.VMEM((3, 1, points), jnp.int32),
            dma((4,)),
            pltpu.VMEM((groups, cap, width), jnp.bfloat16),
            pltpu.VMEM((blocks, groups, cap, width), jnp.bfloat16),
            pltpu.VMEM((groups, 8, LANES), jnp.int32),
            pltpu.VMEM((blocks, groups, 8, LANES), jnp.int32),
            pltpu.VMEM((blocks, slots // LANES, LANES, LANES), jnp.int32),
            pltpu.VMEM((slots // LANES, 8, LANES), jnp.float32),
            pltpu.VMEM((groups, 8, LANES), jnp.float32),
        ]
        + [dma((groups,))] * 10
        + [dma((3,))] * 2
        + [dma((groups,))] * 2,
        compiler_params=pltpu.CompilerParams(
            collective_id=0, has_side_effects=True, vmem_limit_bytes=64 * 1024 * 1024 - 65536
        ),
        cost_estimate=pl.CostEstimate(
            flops=2 * slots * slots * blocks * width, bytes_accessed=points * width * 2, transcendentals=points
        ),
    )(embeddings, point_group.reshape(1, points), point_cluster.reshape(1, points), point_order.reshape(1, points))
    return out


def solution(mesh):
    in_specs = (P(("dp", "blk"), None), P(("dp", "blk"), None), P(("dp", "blk")), P(("dp", "blk")))
    out_specs = P(("dp", "blk"))

    def run(embeddings, point_group, point_cluster, point_order):
        inner = functools.partial(body, embeddings.shape[0])
        return jax.shard_map(inner, mesh=mesh, in_specs=in_specs, out_specs=out_specs, check_vma=False)(
            embeddings, point_group, point_cluster, point_order
        )

    return run
```

```python
import functools

import jax
import jax.numpy as jnp
from jax import lax
from jax.experimental import pallas as pl
from jax.experimental.pallas import tpu as pltpu
from jax.sharding import PartitionSpec as P

CLG = 32
LANES = 128
MESH = pl.DeviceIdType.MESH
NT = (((1,), (1,)), ((), ()))


def flip(index, mask):
    out = index
    bit = 1
    while bit <= mask:
        if mask & bit:
            digit = lax.rem(lax.div(index, jnp.int32(bit)), jnp.int32(2))
            out = out + bit * (1 - 2 * digit)
        bit *= 2
    return out


def kernel(groups, total, order, emb_hbm, group_hbm, cluster_hbm, order_hbm, out_ref, emb_ref, ids, fetched,
           send, keys, msend, meta, kmeta, best, res, back, s1, r1, sm, rm, sy, ry, sc, rc, smx, rmx, sb, rb, s2, r2, s3):
    points, width = emb_ref.shape
    cap = 2 * points // groups
    slots = groups * cap
    per = LANES // cap
    tiles = slots // LANES
    me = lax.axis_index("dp")
    own = lax.axis_index("blk")
    across = {"blk": flip(own, 2)}
    beside = {"blk": flip(own, 1)}
    partner = [None] + [{"dp": flip(me, k)} for k in range(1, groups)]

    fetches = [
        pltpu.make_async_copy(group_hbm, ids.at[0], fetched.at[0]),
        pltpu.make_async_copy(cluster_hbm, ids.at[1], fetched.at[1]),
        pltpu.make_async_copy(order_hbm, ids.at[2], fetched.at[2]),
        pltpu.make_async_copy(emb_hbm, emb_ref, fetched.at[3]),
    ]
    for fetch in fetches:
        fetch.start()

    lead = lax.rem(own, jnp.int32(2)) == 0
    rows_of = [me] + [flip(me, k) for k in range(1, groups)]
    far_y = [{"dp": row, "blk": flip(own, 2)} for row in rows_of]
    far_c = [{"dp": row, "blk": flip(own, 1)} for row in rows_of]
    barrier = pltpu.get_barrier_semaphore()
    for who in partner[1:] + far_y + far_c:
        pl.semaphore_signal(barrier, inc=1, device_id=who, device_id_type=MESH)

    def remote(src, dst, ssem, rsem, who):
        return pltpu.make_async_remote_copy(
            src_ref=src, dst_ref=dst, send_sem=ssem, recv_sem=rsem, device_id=who, device_id_type=MESH
        )

    for fetch in fetches[:3]:
        fetch.wait()
    group = ids[0]
    combined = ids[1] * total + ids[2] + 1
    relative = jnp.bitwise_xor(group, me)
    member = lax.broadcasted_iota(jnp.int32, (groups, points), 0) == relative
    member_f = jnp.where(member, 1.0, 0.0)
    earlier = lax.broadcasted_iota(jnp.int32, (points, points), 0) < lax.broadcasted_iota(
        jnp.int32, (points, points), 1
    )
    before = jnp.dot(
        member_f.astype(jnp.bfloat16),
        jnp.where(earlier, 1.0, 0.0).astype(jnp.bfloat16),
        preferred_element_type=jnp.float32,
    )
    rank = jnp.sum(before * member_f, axis=0, keepdims=True).astype(jnp.int32)
    target = relative * cap + rank

    digits = jnp.concatenate(
        [combined & 127, (combined >> 7) & 127, combined >> 14, jnp.zeros((5, points), jnp.int32)], axis=0
    ).astype(jnp.float32).astype(jnp.bfloat16)
    lane_slot = lax.broadcasted_iota(jnp.int32, (LANES, points), 0) & (cap - 1)
    local_target = target & (cap - 1)
    same_rank = lane_slot == local_target
    for k in range(groups):
        pick = jnp.where(same_rank & (relative == k), 1.0, 0.0).astype(jnp.bfloat16)
        got = lax.dot_general(digits, pick, NT, preferred_element_type=jnp.float32)
        row = got[0:1, :] + 128.0 * got[1:2, :] + 16384.0 * got[2:3, :]
        row = jnp.broadcast_to(row.astype(jnp.int32), (8, LANES))
        if k == 0:
            meta[0, 0] = row
        else:
            msend[k] = row

    fetches[3].wait()
    values = emb_ref[...].astype(jnp.float32)
    scale = lax.rsqrt(jnp.mean(values * values, axis=1, keepdims=True) + 1e-06)
    unit = (values * scale * width ** (-0.5)).astype(jnp.bfloat16)

    pl.semaphore_wait(barrier, 3 * groups - 1)

    started = []
    meta_copies = [None] * groups
    for k in order:
        meta_copies[k] = remote(msend.at[k], meta.at[0, k], sm.at[k], rm.at[k], partner[k])
        meta_copies[k].start()

    first = [None] * groups
    over_y = [None] * groups
    over_c = [None] * groups

    def forward(k):
        over_y[k] = remote(keys.at[0, k], keys.at[2, k], sy.at[k], ry.at[k], across)
        over_y[k].start()
        over_c[k] = remote(keys.at[0, k], keys.at[1, k], sc.at[k], rc.at[k], beside)
        pl.when(jnp.logical_not(lead))(over_c[k].start)

    slot_rows = lax.broadcasted_iota(jnp.int32, (cap, points), 0)
    for k in [order[0], 0] + list(order[1:]):
        place = jnp.where(slot_rows + k * cap == target, 1.0, 0.0).astype(jnp.bfloat16)
        rows = jnp.dot(place, unit, preferred_element_type=jnp.float32).astype(jnp.bfloat16)
        if k == 0:
            keys[0, 0] = rows
            forward(0)
        else:
            send[k] = rows
            first[k] = remote(send.at[k], keys.at[0, k], s1.at[k], r1.at[k], partner[k])
            first[k].start()

    def key_rows(r):
        lane_block = lax.broadcasted_iota(jnp.int32, (1, LANES), 1) // cap
        rows = []
        for t in range(tiles):
            row = meta[r, t * per][0:1, :]
            for j in range(1, per):
                row = jnp.where(lane_block == j, meta[r, t * per + j][0:1, :], row)
            rows.append(row)
        return rows

    def key_tiles(r):
        for t, row in enumerate(key_rows(r)):
            kmeta[r, t] = jnp.broadcast_to(row, (LANES, LANES)).T

    for k in order:
        meta_copies[k].wait_recv()
    meta_y = remote(meta.at[0], meta.at[2], smx.at[0], rmx.at[0], across)
    meta_y.start()
    meta_c = remote(meta.at[0], meta.at[1], smx.at[1], rmx.at[1], beside)
    meta_c.start()
    key_tiles(0)
    best[...] = jnp.full_like(best, -2.0)

    for k in order:
        first[k].wait_recv()
        forward(k)
    meta_y.wait_recv()
    key_tiles(2)
    meta_c.wait_recv()
    key_tiles(1)

    half = tiles // 2

    def visit(q, r):
        queries = keys[q].reshape(slots, width)
        query = jnp.concatenate(key_rows(q), axis=1)
        floor = (query - 1) & (-total)
        found = best[q]
        for h in range(2):
            block = keys[r, h * (groups // 2):(h + 1) * (groups // 2)].reshape(slots // 2, width)
            scores = lax.dot_general(block, queries, NT, preferred_element_type=jnp.float32)
            for t in range(half):
                mine = jnp.concatenate([kmeta[r, h * half + t]] * tiles, axis=1)
                part = jnp.where((mine < query) & (mine > floor), scores[t * LANES:(t + 1) * LANES], -2.0)
                found = jnp.maximum(found, jnp.max(part.reshape(LANES // 8, 8, slots), axis=0))
        best[q] = found

    def answer(q):
        found = jnp.max(best[q], axis=0, keepdims=True)
        found = jnp.broadcast_to(found, (8, slots))
        for t in range(tiles):
            res[q, t] = found[:, t * LANES:(t + 1) * LANES]

    visit(0, 0)

    @pl.when(lead)
    def _():
        for k in range(groups):
            over_c[k].wait_recv()
        visit(1, 0)
        visit(0, 1)

    for k in range(groups):
        over_y[k].wait_recv()

    extra_y = [remote(res.at[2, k // per], back.at[1, k], s2.at[k], r2.at[k], far_y[k]) for k in range(groups)]
    extra_c = [remote(res.at[1, k // per], back.at[1, k], s3.at[k], r2.at[k], far_c[k]) for k in range(groups)]

    @pl.when(lead)
    def _():
        visit(2, 1)
        answer(2)
        for copy in extra_y:
            copy.start()
        visit(1, 2)
        answer(1)
        for copy in extra_c:
            copy.start()

    visit(0, 2)
    answer(0)
    back[0, 0] = res[0, 0]
    replies = [None] * groups
    for k in order:
        replies[k] = remote(res.at[0, k // per], back.at[0, k], sb.at[k], rb.at[k], partner[k])
        replies[k].start()

    for k in range(groups):
        over_y[k].wait_send()
        if k:
            first[k].wait_send()
            meta_copies[k].wait_send()
    meta_y.wait_send()
    meta_c.wait_send()

    @pl.when(jnp.logical_not(lead))
    def _():
        for k in range(groups):
            over_c[k].wait_send()

    lane_block = lax.broadcasted_iota(jnp.int32, (1, LANES), 1) // cap
    nearest = jnp.full((1, points), -2.0, jnp.float32)
    slot_iota = lax.broadcasted_iota(jnp.int32, (LANES, points), 0)
    for t in range(tiles):
        for j in range(per):
            if t * per + j:
                replies[t * per + j].wait_recv()
            extra_y[t * per + j].wait_recv()
        row = jnp.maximum(back[0, t * per], back[1, t * per])[0:1, :]
        for j in range(1, per):
            pair = jnp.maximum(back[0, t * per + j], back[1, t * per + j])
            row = jnp.where(lane_block == j, pair[0:1, :], row)
        column = jnp.broadcast_to(row, (LANES, LANES)).T
        column = jnp.concatenate([column] * (points // LANES), axis=1)
        hit = jnp.where(slot_iota + t * LANES == target, column, -2.0)
        nearest = jnp.maximum(nearest, jnp.max(hit, axis=0, keepdims=True))
    out_ref[...] = jnp.where(nearest > -1.5, nearest, -1.0).reshape(points)
    for k in order:
        replies[k].wait_send()

    @pl.when(lead)
    def _():
        for k in range(groups):
            extra_y[k].wait_send()
            extra_c[k].wait_send()


def body(total, embeddings, point_group, point_cluster, point_order):
    groups = lax.axis_size("dp")
    blocks = lax.axis_size("blk")
    points, width = embeddings.shape
    cap = 2 * points // groups
    slots = groups * cap
    near, far = list(range(1, groups // 2)), list(range(groups // 2, groups))
    order = [k for pair in zip(near, far) for k in pair] + far[len(near):]
    dma = pltpu.SemaphoreType.DMA
    out = pl.pallas_call(
        functools.partial(kernel, groups, total, order),
        out_shape=jax.ShapeDtypeStruct((points,), jnp.float32),
        in_specs=[pl.BlockSpec(memory_space=pl.ANY)] * 4,
        out_specs=pl.BlockSpec(memory_space=pltpu.VMEM),
        scratch_shapes=[
            pltpu.VMEM((points, width), jnp.bfloat16),
            pltpu.VMEM((3, 1, points), jnp.int32),
            dma((4,)),
            pltpu.VMEM((groups, cap, width), jnp.bfloat16),
            pltpu.VMEM((3, groups, cap, width), jnp.bfloat16),
            pltpu.VMEM((groups, 8, LANES), jnp.int32),
            pltpu.VMEM((3, groups, 8, LANES), jnp.int32),
            pltpu.VMEM((3, slots // LANES, LANES, LANES), jnp.int32),
            pltpu.VMEM((3, 8, slots), jnp.float32),
            pltpu.VMEM((3, slots // LANES, 8, LANES), jnp.float32),
            pltpu.VMEM((2, groups, 8, LANES), jnp.float32),
        ]
        + [dma((groups,))] * 8
        + [dma((2,))] * 2
        + [dma((groups,))] * 5,
        compiler_params=pltpu.CompilerParams(
            collective_id=0, has_side_effects=True, vmem_limit_bytes=64 * 1024 * 1024 - 65536
        ),
        cost_estimate=pl.CostEstimate(
            flops=2 * slots * slots * blocks * width, bytes_accessed=points * width * 2, transcendentals=points
        ),
    )(embeddings, point_group.reshape(1, points), point_cluster.reshape(1, points), point_order.reshape(1, points))
    return out


def solution(mesh):
    in_specs = (P(("dp", "blk"), None), P(("dp", "blk"), None), P(("dp", "blk")), P(("dp", "blk")))
    out_specs = P(("dp", "blk"))

    def run(embeddings, point_group, point_cluster, point_order):
        inner = functools.partial(body, embeddings.shape[0])
        return jax.shard_map(inner, mesh=mesh, in_specs=in_specs, out_specs=out_specs, check_vma=False)(
            embeddings, point_group, point_cluster, point_order
        )

    return run
```

```python
import functools

import jax
import jax.numpy as jnp
from jax import lax
from jax.experimental import pallas as pl
from jax.experimental.pallas import tpu as pltpu
from jax.sharding import PartitionSpec as P

CLG = 32
LANES = 128
MESH = pl.DeviceIdType.MESH
NT = (((1,), (1,)), ((), ()))


def flip(index, mask):
    out = index
    bit = 1
    while bit <= mask:
        if mask & bit:
            digit = lax.rem(lax.div(index, jnp.int32(bit)), jnp.int32(2))
            out = out + bit * (1 - 2 * digit)
        bit *= 2
    return out


def kernel(groups, total, order, emb_hbm, group_hbm, cluster_hbm, order_hbm, out_ref, emb_ref, ids, fetched,
           send, keys, msend, meta, kmeta, best, res, back, s1, r1, sm, rm, sy, ry, sc, rc, smx, rmx, sb, rb, s2, r2, s3):
    points, width = emb_ref.shape
    cap = 2 * points // groups
    slots = groups * cap
    per = LANES // cap
    tiles = slots // LANES
    me = lax.axis_index("dp")
    own = lax.axis_index("blk")
    across = {"blk": flip(own, 2)}
    beside = {"blk": flip(own, 1)}
    partner = [None] + [{"dp": flip(me, k)} for k in range(1, groups)]

    fetches = [
        pltpu.make_async_copy(group_hbm, ids.at[0], fetched.at[0]),
        pltpu.make_async_copy(cluster_hbm, ids.at[1], fetched.at[1]),
        pltpu.make_async_copy(order_hbm, ids.at[2], fetched.at[2]),
        pltpu.make_async_copy(emb_hbm, emb_ref, fetched.at[3]),
    ]
    for fetch in fetches:
        fetch.start()

    lead = lax.rem(own, jnp.int32(2)) == 0
    rows_of = [me] + [flip(me, k) for k in range(1, groups)]
    far_y = [{"dp": row, "blk": flip(own, 2)} for row in rows_of]
    far_c = [{"dp": row, "blk": flip(own, 1)} for row in rows_of]
    barrier = pltpu.get_barrier_semaphore()
    for who in partner[1:] + far_y + far_c:
        pl.semaphore_signal(barrier, inc=1, device_id=who, device_id_type=MESH)

    def remote(src, dst, ssem, rsem, who):
        return pltpu.make_async_remote_copy(
            src_ref=src, dst_ref=dst, send_sem=ssem, recv_sem=rsem, device_id=who, device_id_type=MESH
        )

    for fetch in fetches[:3]:
        fetch.wait()
    group = ids[0]
    combined = ids[1] * total + ids[2] + 1
    relative = jnp.bitwise_xor(group, me)
    member = lax.broadcasted_iota(jnp.int32, (groups, points), 0) == relative
    member_f = jnp.where(member, 1.0, 0.0)
    earlier = lax.broadcasted_iota(jnp.int32, (points, points), 0) < lax.broadcasted_iota(
        jnp.int32, (points, points), 1
    )
    before = jnp.dot(
        member_f.astype(jnp.bfloat16),
        jnp.where(earlier, 1.0, 0.0).astype(jnp.bfloat16),
        preferred_element_type=jnp.float32,
    )
    rank = jnp.sum(before * member_f, axis=0, keepdims=True).astype(jnp.int32)
    target = relative * cap + rank

    digits = jnp.concatenate(
        [combined & 127, (combined >> 7) & 127, combined >> 14, jnp.zeros((5, points), jnp.int32)], axis=0
    ).astype(jnp.float32).astype(jnp.bfloat16)
    lane_slot = lax.broadcasted_iota(jnp.int32, (LANES, points), 0) & (cap - 1)
    local_target = target & (cap - 1)
    same_rank = lane_slot == local_target
    for k in range(groups):
        pick = jnp.where(same_rank & (relative == k), 1.0, 0.0).astype(jnp.bfloat16)
        got = lax.dot_general(digits, pick, NT, preferred_element_type=jnp.float32)
        row = got[0:1, :] + 128.0 * got[1:2, :] + 16384.0 * got[2:3, :]
        row = jnp.broadcast_to(row.astype(jnp.int32), (8, LANES))
        if k == 0:
            meta[0, 0] = row
        else:
            msend[k] = row

    fetches[3].wait()
    values = emb_ref[...].astype(jnp.float32)
    scale = lax.rsqrt(jnp.mean(values * values, axis=1, keepdims=True) + 1e-06)
    unit = (values * scale * width ** (-0.5)).astype(jnp.bfloat16)

    pl.semaphore_wait(barrier, 3 * groups - 1)

    started = []
    meta_copies = [None] * groups
    for k in order:
        meta_copies[k] = remote(msend.at[k], meta.at[0, k], sm.at[k], rm.at[k], partner[k])
        meta_copies[k].start()

    first = [None] * groups
    over_y = [None] * groups
    over_c = [None] * groups

    def forward(k):
        over_y[k] = remote(keys.at[0, k], keys.at[2, k], sy.at[k], ry.at[k], across)
        over_y[k].start()
        over_c[k] = remote(keys.at[0, k], keys.at[1, k], sc.at[k], rc.at[k], beside)
        pl.when(jnp.logical_not(lead))(over_c[k].start)

    slot_rows = lax.broadcasted_iota(jnp.int32, (cap, points), 0)
    for k in [order[0], 0] + list(order[1:]):
        place = jnp.where(slot_rows + k * cap == target, 1.0, 0.0).astype(jnp.bfloat16)
        rows = jnp.dot(place, unit, preferred_element_type=jnp.float32).astype(jnp.bfloat16)
        if k == 0:
            keys[0, 0] = rows
            forward(0)
        else:
            send[k] = rows
            first[k] = remote(send.at[k], keys.at[0, k], s1.at[k], r1.at[k], partner[k])
            first[k].start()

    def key_rows(r):
        lane_block = lax.broadcasted_iota(jnp.int32, (1, LANES), 1) // cap
        rows = []
        for t in range(tiles):
            row = meta[r, t * per][0:1, :]
            for j in range(1, per):
                row = jnp.where(lane_block == j, meta[r, t * per + j][0:1, :], row)
            rows.append(row)
        return rows

    def key_tiles(r):
        for t, row in enumerate(key_rows(r)):
            kmeta[r, t] = jnp.broadcast_to(row, (LANES, LANES)).T

    for k in order:
        meta_copies[k].wait_recv()
    meta_y = remote(meta.at[0], meta.at[2], smx.at[0], rmx.at[0], across)
    meta_y.start()
    meta_c = remote(meta.at[0], meta.at[1], smx.at[1], rmx.at[1], beside)
    meta_c.start()
    key_tiles(0)
    best[...] = jnp.full_like(best, -2.0)

    middle, half = groups // 2, tiles // 2
    both, near, far = (0, tiles), (0, half), (half, tiles)

    def visit(q, r, q_span, r_span):
        (q0, q1), (r0, r1) = q_span, r_span
        wide = (q1 - q0) * LANES
        queries = keys[q, q0 * per:q1 * per].reshape(wide, width)
        query = jnp.concatenate(key_rows(q)[q0:q1], axis=1)
        floor = (query - 1) & (-total)
        found = best[q, :, q0 * LANES:q1 * LANES]
        for t0 in range(r0, r1, half):
            block = keys[r, t0 * per:(t0 + half) * per].reshape(half * LANES, width)
            scores = lax.dot_general(block, queries, NT, preferred_element_type=jnp.float32)
            for t in range(half):
                mine = jnp.concatenate([kmeta[r, t0 + t]] * (q1 - q0), axis=1)
                part = jnp.where((mine < query) & (mine > floor), scores[t * LANES:(t + 1) * LANES], -2.0)
                found = jnp.maximum(found, jnp.max(part.reshape(LANES // 8, 8, wide), axis=0))
        best[q, :, q0 * LANES:q1 * LANES] = found

    def answer(q):
        found = jnp.max(best[q], axis=0, keepdims=True)
        found = jnp.broadcast_to(found, (8, slots))
        for t in range(tiles):
            res[q, t] = found[:, t * LANES:(t + 1) * LANES]

    for k in order:
        first[k].wait_recv()
        forward(k)
        if k == middle - 1:
            meta_y.wait_recv()
            key_tiles(2)
            meta_c.wait_recv()
            key_tiles(1)
            visit(0, 0, near, near)
    visit(0, 0, far, near)
    visit(0, 0, both, far)

    @pl.when(lead)
    def _():
        for k in range(middle):
            over_c[k].wait_recv()
        visit(1, 0, near, both)
        visit(0, 1, both, near)

    for k in range(middle):
        over_y[k].wait_recv()
    visit(0, 2, both, near)

    @pl.when(lead)
    def _():
        visit(2, 1, near, near)
        visit(1, 2, near, near)
        for k in range(middle, groups):
            over_c[k].wait_recv()
        visit(1, 0, far, both)
        visit(0, 1, both, far)
        visit(2, 1, near, far)
        visit(1, 2, far, near)

    for k in range(middle, groups):
        over_y[k].wait_recv()

    extra_y = [remote(res.at[2, k // per], back.at[1, k], s2.at[k], r2.at[k], far_y[k]) for k in range(groups)]
    extra_c = [remote(res.at[1, k // per], back.at[1, k], s3.at[k], r2.at[k], far_c[k]) for k in range(groups)]

    @pl.when(lead)
    def _():
        visit(2, 1, far, both)
        answer(2)
        for copy in extra_y:
            copy.start()
        visit(1, 2, both, far)
        answer(1)
        for copy in extra_c:
            copy.start()

    visit(0, 2, both, far)
    answer(0)
    back[0, 0] = res[0, 0]
    replies = [None] * groups
    for k in order:
        replies[k] = remote(res.at[0, k // per], back.at[0, k], sb.at[k], rb.at[k], partner[k])
        replies[k].start()

    for k in range(groups):
        over_y[k].wait_send()
        if k:
            first[k].wait_send()
            meta_copies[k].wait_send()
    meta_y.wait_send()
    meta_c.wait_send()

    @pl.when(jnp.logical_not(lead))
    def _():
        for k in range(groups):
            over_c[k].wait_send()

    lane_block = lax.broadcasted_iota(jnp.int32, (1, LANES), 1) // cap
    nearest = jnp.full((1, points), -2.0, jnp.float32)
    slot_iota = lax.broadcasted_iota(jnp.int32, (LANES, points), 0)
    for t in range(tiles):
        for j in range(per):
            if t * per + j:
                replies[t * per + j].wait_recv()
            extra_y[t * per + j].wait_recv()
        row = jnp.maximum(back[0, t * per], back[1, t * per])[0:1, :]
        for j in range(1, per):
            pair = jnp.maximum(back[0, t * per + j], back[1, t * per + j])
            row = jnp.where(lane_block == j, pair[0:1, :], row)
        column = jnp.broadcast_to(row, (LANES, LANES)).T
        column = jnp.concatenate([column] * (points // LANES), axis=1)
        hit = jnp.where(slot_iota + t * LANES == target, column, -2.0)
        nearest = jnp.maximum(nearest, jnp.max(hit, axis=0, keepdims=True))
    out_ref[...] = jnp.where(nearest > -1.5, nearest, -1.0).reshape(points)
    for k in order:
        replies[k].wait_send()

    @pl.when(lead)
    def _():
        for k in range(groups):
            extra_y[k].wait_send()
            extra_c[k].wait_send()


def body(total, embeddings, point_group, point_cluster, point_order):
    groups = lax.axis_size("dp")
    blocks = lax.axis_size("blk")
    points, width = embeddings.shape
    cap = 2 * points // groups
    slots = groups * cap
    near, far = list(range(1, groups // 2)), list(range(groups // 2, groups))
    order = [k for pair in zip(near, far) for k in pair] + far[len(near):]
    dma = pltpu.SemaphoreType.DMA
    out = pl.pallas_call(
        functools.partial(kernel, groups, total, order),
        out_shape=jax.ShapeDtypeStruct((points,), jnp.float32),
        in_specs=[pl.BlockSpec(memory_space=pl.ANY)] * 4,
        out_specs=pl.BlockSpec(memory_space=pltpu.VMEM),
        scratch_shapes=[
            pltpu.VMEM((points, width), jnp.bfloat16),
            pltpu.VMEM((3, 1, points), jnp.int32),
            dma((4,)),
            pltpu.VMEM((groups, cap, width), jnp.bfloat16),
            pltpu.VMEM((3, groups, cap, width), jnp.bfloat16),
            pltpu.VMEM((groups, 8, LANES), jnp.int32),
            pltpu.VMEM((3, groups, 8, LANES), jnp.int32),
            pltpu.VMEM((3, slots // LANES, LANES, LANES), jnp.int32),
            pltpu.VMEM((3, 8, slots), jnp.float32),
            pltpu.VMEM((3, slots // LANES, 8, LANES), jnp.float32),
            pltpu.VMEM((2, groups, 8, LANES), jnp.float32),
        ]
        + [dma((groups,))] * 8
        + [dma((2,))] * 2
        + [dma((groups,))] * 5,
        compiler_params=pltpu.CompilerParams(
            collective_id=0, has_side_effects=True, vmem_limit_bytes=64 * 1024 * 1024 - 65536
        ),
        cost_estimate=pl.CostEstimate(
            flops=2 * slots * slots * blocks * width, bytes_accessed=points * width * 2, transcendentals=points
        ),
    )(embeddings, point_group.reshape(1, points), point_cluster.reshape(1, points), point_order.reshape(1, points))
    return out


def solution(mesh):
    in_specs = (P(("dp", "blk"), None), P(("dp", "blk"), None), P(("dp", "blk")), P(("dp", "blk")))
    out_specs = P(("dp", "blk"))

    def run(embeddings, point_group, point_cluster, point_order):
        inner = functools.partial(body, embeddings.shape[0])
        return jax.shard_map(inner, mesh=mesh, in_specs=in_specs, out_specs=out_specs, check_vma=False)(
            embeddings, point_group, point_cluster, point_order
        )

    return run
```

```python
import functools

import jax
import jax.numpy as jnp
from jax import lax
from jax.experimental import pallas as pl
from jax.experimental.pallas import tpu as pltpu
from jax.sharding import PartitionSpec as P

CLG = 32
LANES = 128
MESH = pl.DeviceIdType.MESH
NT = (((1,), (1,)), ((), ()))


def flip(index, mask):
    out = index
    bit = 1
    while bit <= mask:
        if mask & bit:
            digit = lax.rem(lax.div(index, jnp.int32(bit)), jnp.int32(2))
            out = out + bit * (1 - 2 * digit)
        bit *= 2
    return out


def kernel(groups, total, order, emb_hbm, group_hbm, cluster_hbm, order_hbm, out_ref, emb_ref, ids, fetched,
           send, keys, msend, meta, kmeta, best, res, back, s1, r1, sm, rm, sy, ry, sc, rc, smx, rmx, sb, rb, s2, r2, s3):
    points, width = emb_ref.shape
    cap = 2 * points // groups
    slots = groups * cap
    per = LANES // cap
    tiles = slots // LANES
    me = lax.axis_index("dp")
    own = lax.axis_index("blk")
    across = {"blk": flip(own, 2)}
    beside = {"blk": flip(own, 1)}
    partner = [None] + [{"dp": flip(me, k)} for k in range(1, groups)]

    fetches = [
        pltpu.make_async_copy(group_hbm, ids.at[0], fetched.at[0]),
        pltpu.make_async_copy(cluster_hbm, ids.at[1], fetched.at[1]),
        pltpu.make_async_copy(order_hbm, ids.at[2], fetched.at[2]),
        pltpu.make_async_copy(emb_hbm, emb_ref, fetched.at[3]),
    ]
    for fetch in fetches:
        fetch.start()

    lead = lax.rem(own, jnp.int32(2)) == 0
    rows_of = [me] + [flip(me, k) for k in range(1, groups)]
    far_y = [{"dp": row, "blk": flip(own, 2)} for row in rows_of]
    far_c = [{"dp": row, "blk": flip(own, 1)} for row in rows_of]
    barrier = pltpu.get_barrier_semaphore()
    for who in partner[1:] + far_y + far_c:
        pl.semaphore_signal(barrier, inc=1, device_id=who, device_id_type=MESH)

    def remote(src, dst, ssem, rsem, who):
        return pltpu.make_async_remote_copy(
            src_ref=src, dst_ref=dst, send_sem=ssem, recv_sem=rsem, device_id=who, device_id_type=MESH
        )

    for fetch in fetches[:3]:
        fetch.wait()
    group = ids[0]
    combined = ids[1] * total + ids[2] + 1
    relative = jnp.bitwise_xor(group, me)
    member = lax.broadcasted_iota(jnp.int32, (groups, points), 0) == relative
    member_f = jnp.where(member, 1.0, 0.0)
    earlier = lax.broadcasted_iota(jnp.int32, (points, points), 0) < lax.broadcasted_iota(
        jnp.int32, (points, points), 1
    )
    before = jnp.dot(
        member_f.astype(jnp.bfloat16),
        jnp.where(earlier, 1.0, 0.0).astype(jnp.bfloat16),
        preferred_element_type=jnp.float32,
    )
    rank = jnp.sum(before * member_f, axis=0, keepdims=True).astype(jnp.int32)
    target = relative * cap + rank

    digits = jnp.concatenate(
        [combined & 127, (combined >> 7) & 127, combined >> 14, jnp.zeros((5, points), jnp.int32)], axis=0
    ).astype(jnp.float32).astype(jnp.bfloat16)
    lane_row = lax.broadcasted_iota(jnp.int32, (groups * LANES, points), 0)
    lane_slot = (lane_row // LANES) * cap + (lane_row & (cap - 1))
    pick = jnp.where(lane_slot == target, 1.0, 0.0).astype(jnp.bfloat16)
    got = lax.dot_general(digits, pick, NT, preferred_element_type=jnp.float32)
    row = got[0:1, :] + 128.0 * got[1:2, :] + 16384.0 * got[2:3, :]
    row = jnp.broadcast_to(row.astype(jnp.int32), (8, groups * LANES))
    meta[0, 0] = row[:, :LANES]
    for k in range(1, groups):
        msend[k] = row[:, k * LANES:(k + 1) * LANES]

    fetches[3].wait()
    values = emb_ref[...].astype(jnp.float32)
    scale = lax.rsqrt(jnp.mean(values * values, axis=1, keepdims=True) + 1e-06)
    unit = (values * scale * width ** (-0.5)).astype(jnp.bfloat16)

    pl.semaphore_wait(barrier, 3 * groups - 1)

    started = []
    meta_copies = [None] * groups
    for k in order:
        meta_copies[k] = remote(msend.at[k], meta.at[0, k], sm.at[k], rm.at[k], partner[k])
        meta_copies[k].start()

    first = [None] * groups
    over_y = [None] * groups
    over_c = [None] * groups

    def forward(k):
        over_y[k] = remote(keys.at[0, k], keys.at[2, k], sy.at[k], ry.at[k], across)
        over_y[k].start()
        over_c[k] = remote(keys.at[0, k], keys.at[1, k], sc.at[k], rc.at[k], beside)
        pl.when(jnp.logical_not(lead))(over_c[k].start)

    slot_rows = lax.broadcasted_iota(jnp.int32, (cap, points), 0)
    plans = [[order[0], 0] + list(order[1:]), [order[1], order[0], 0, order[3], order[2]] + list(order[4:])]
    ready = []
    for k in [order[0], order[1], 0, order[3], order[2]] + list(order[4:]):
        place = jnp.where(slot_rows + k * cap == target, 1.0, 0.0).astype(jnp.bfloat16)
        rows = jnp.dot(place, unit, preferred_element_type=jnp.float32).astype(jnp.bfloat16)
        if k == 0:
            keys[0, 0] = rows
        else:
            send[k] = rows
            first[k] = remote(send.at[k], keys.at[0, k], s1.at[k], r1.at[k], partner[k])
        ready.append(k)
        if len(ready) == 1:
            continue
        for plan, mine in zip(plans, (lead, jnp.logical_not(lead))):
            go = []
            while plan and plan[0] in ready:
                go.append(plan.pop(0))

            @pl.when(mine)
            def _(go=tuple(go)):
                for j in go:
                    if j:
                        first[j].start()

        if k == 0:
            forward(0)

    def key_rows(r):
        lane_block = lax.broadcasted_iota(jnp.int32, (1, LANES), 1) // cap
        rows = []
        for t in range(tiles):
            row = meta[r, t * per][0:1, :]
            for j in range(1, per):
                row = jnp.where(lane_block == j, meta[r, t * per + j][0:1, :], row)
            rows.append(row)
        return rows

    def key_tiles(r):
        for t, row in enumerate(key_rows(r)):
            kmeta[r, t] = jnp.broadcast_to(row, (LANES, LANES)).T

    for k in order:
        meta_copies[k].wait_recv()
    meta_y = remote(meta.at[0], meta.at[2], smx.at[0], rmx.at[0], across)
    meta_y.start()
    meta_c = remote(meta.at[0], meta.at[1], smx.at[1], rmx.at[1], beside)
    meta_c.start()
    key_tiles(0)
    best[...] = jnp.full_like(best, -2.0)

    middle, half = groups // 2, tiles // 2
    both, near, far = (0, tiles), (0, half), (half, tiles)

    def visit(q, r, q_span, r_span):
        (q0, q1), (r0, r1) = q_span, r_span
        wide = (q1 - q0) * LANES
        queries = keys[q, q0 * per:q1 * per].reshape(wide, width)
        query = jnp.concatenate(key_rows(q)[q0:q1], axis=1)
        floor = (query - 1) & (-total)
        found = best[q, :, q0 * LANES:q1 * LANES]
        for t0 in range(r0, r1, half):
            block = keys[r, t0 * per:(t0 + half) * per].reshape(half * LANES, width)
            scores = lax.dot_general(block, queries, NT, preferred_element_type=jnp.float32)
            for t in range(half):
                mine = jnp.concatenate([kmeta[r, t0 + t]] * (q1 - q0), axis=1)
                part = jnp.where((mine < query) & (mine > floor), scores[t * LANES:(t + 1) * LANES], -2.0)
                found = jnp.maximum(found, jnp.max(part.reshape(LANES // 8, 8, wide), axis=0))
        best[q, :, q0 * LANES:q1 * LANES] = found

    def answer(q):
        found = jnp.max(best[q], axis=0, keepdims=True)
        found = jnp.broadcast_to(found, (8, slots))
        for t in range(tiles):
            res[q, t] = found[:, t * LANES:(t + 1) * LANES]

    for k in order:
        first[k].wait_recv()
        forward(k)
        if k == middle - 1:
            meta_y.wait_recv()
            key_tiles(2)
            meta_c.wait_recv()
            key_tiles(1)
            visit(0, 0, near, near)
    visit(0, 0, far, near)
    visit(0, 0, both, far)

    @pl.when(lead)
    def _():
        for k in range(middle):
            over_c[k].wait_recv()
        visit(1, 0, near, both)
        visit(0, 1, both, near)

    for k in range(middle):
        over_y[k].wait_recv()
    visit(0, 2, both, near)

    @pl.when(lead)
    def _():
        visit(2, 1, near, near)
        visit(1, 2, near, near)
        for k in range(middle, groups):
            over_c[k].wait_recv()
        visit(1, 0, far, both)
        visit(0, 1, both, far)
        visit(2, 1, near, far)
        visit(1, 2, far, near)

    for k in range(middle, groups):
        over_y[k].wait_recv()

    extra_y = [remote(res.at[2, k // per], back.at[1, k], s2.at[k], r2.at[k], far_y[k]) for k in range(groups)]
    extra_c = [remote(res.at[1, k // per], back.at[1, k], s3.at[k], r2.at[k], far_c[k]) for k in range(groups)]

    @pl.when(lead)
    def _():
        visit(2, 1, far, both)
        answer(2)
        for copy in extra_y:
            copy.start()
        visit(1, 2, both, far)
        answer(1)
        for copy in extra_c:
            copy.start()

    visit(0, 2, both, far)
    answer(0)
    back[0, 0] = res[0, 0]
    replies = [None] * groups
    for k in order:
        replies[k] = remote(res.at[0, k // per], back.at[0, k], sb.at[k], rb.at[k], partner[k])
        replies[k].start()

    for k in range(groups):
        over_y[k].wait_send()
        if k:
            first[k].wait_send()
            meta_copies[k].wait_send()
    meta_y.wait_send()
    meta_c.wait_send()

    @pl.when(jnp.logical_not(lead))
    def _():
        for k in range(groups):
            over_c[k].wait_send()

    lane_block = lax.broadcasted_iota(jnp.int32, (1, LANES), 1) // cap
    nearest = jnp.full((1, points), -2.0, jnp.float32)
    slot_iota = lax.broadcasted_iota(jnp.int32, (LANES, points), 0)
    for t in range(tiles):
        for j in range(per):
            if t * per + j:
                replies[t * per + j].wait_recv()
            extra_y[t * per + j].wait_recv()
        row = jnp.maximum(back[0, t * per], back[1, t * per])[0:1, :]
        for j in range(1, per):
            pair = jnp.maximum(back[0, t * per + j], back[1, t * per + j])
            row = jnp.where(lane_block == j, pair[0:1, :], row)
        column = jnp.broadcast_to(row, (LANES, LANES)).T
        column = jnp.concatenate([column] * (points // LANES), axis=1)
        hit = jnp.where(slot_iota + t * LANES == target, column, -2.0)
        nearest = jnp.maximum(nearest, jnp.max(hit, axis=0, keepdims=True))
    out_ref[...] = jnp.where(nearest > -1.5, nearest, -1.0).reshape(points)
    for k in order:
        replies[k].wait_send()

    @pl.when(lead)
    def _():
        for k in range(groups):
            extra_y[k].wait_send()
            extra_c[k].wait_send()


def body(total, embeddings, point_group, point_cluster, point_order):
    groups = lax.axis_size("dp")
    blocks = lax.axis_size("blk")
    points, width = embeddings.shape
    cap = 2 * points // groups
    slots = groups * cap
    near, far = list(range(1, groups // 2)), list(range(groups // 2, groups))
    order = [k for pair in zip(near, far) for k in pair] + far[len(near):]
    dma = pltpu.SemaphoreType.DMA
    out = pl.pallas_call(
        functools.partial(kernel, groups, total, order),
        out_shape=jax.ShapeDtypeStruct((points,), jnp.float32),
        in_specs=[pl.BlockSpec(memory_space=pl.ANY)] * 4,
        out_specs=pl.BlockSpec(memory_space=pltpu.VMEM),
        scratch_shapes=[
            pltpu.VMEM((points, width), jnp.bfloat16),
            pltpu.VMEM((3, 1, points), jnp.int32),
            dma((4,)),
            pltpu.VMEM((groups, cap, width), jnp.bfloat16),
            pltpu.VMEM((3, groups, cap, width), jnp.bfloat16),
            pltpu.VMEM((groups, 8, LANES), jnp.int32),
            pltpu.VMEM((3, groups, 8, LANES), jnp.int32),
            pltpu.VMEM((3, slots // LANES, LANES, LANES), jnp.int32),
            pltpu.VMEM((3, 8, slots), jnp.float32),
            pltpu.VMEM((3, slots // LANES, 8, LANES), jnp.float32),
            pltpu.VMEM((2, groups, 8, LANES), jnp.float32),
        ]
        + [dma((groups,))] * 8
        + [dma((2,))] * 2
        + [dma((groups,))] * 5,
        compiler_params=pltpu.CompilerParams(
            collective_id=0, has_side_effects=True, vmem_limit_bytes=64 * 1024 * 1024 - 65536
        ),
        cost_estimate=pl.CostEstimate(
            flops=2 * slots * slots * blocks * width, bytes_accessed=points * width * 2, transcendentals=points
        ),
    )(embeddings, point_group.reshape(1, points), point_cluster.reshape(1, points), point_order.reshape(1, points))
    return out


def solution(mesh):
    in_specs = (P(("dp", "blk"), None), P(("dp", "blk"), None), P(("dp", "blk")), P(("dp", "blk")))
    out_specs = P(("dp", "blk"))

    def run(embeddings, point_group, point_cluster, point_order):
        inner = functools.partial(body, embeddings.shape[0])
        return jax.shard_map(inner, mesh=mesh, in_specs=in_specs, out_specs=out_specs, check_vma=False)(
            embeddings, point_group, point_cluster, point_order
        )

    return run
```

```python
import functools

import jax
import jax.numpy as jnp
from jax import lax
from jax.experimental import pallas as pl
from jax.experimental.pallas import tpu as pltpu
from jax.sharding import PartitionSpec as P

CLG = 32
LANES = 128
MESH = pl.DeviceIdType.MESH
NT = (((1,), (1,)), ((), ()))


def flip(index, mask):
    out = index
    bit = 1
    while bit <= mask:
        if mask & bit:
            digit = lax.rem(lax.div(index, jnp.int32(bit)), jnp.int32(2))
            out = out + bit * (1 - 2 * digit)
        bit *= 2
    return out


def kernel(groups, total, order, emb_hbm, group_hbm, cluster_hbm, order_hbm, out_ref, emb_ref, ids, fetched,
           send, keys, msend, meta, kmeta, best, res, back, s1, r1, sm, rm, sy, ry, sc, rc, smx, rmx, sb, rb, s2, r2, s3):
    points, width = emb_ref.shape
    cap = 2 * points // groups
    slots = groups * cap
    per = LANES // cap
    tiles = slots // LANES
    me = lax.axis_index("dp")
    own = lax.axis_index("blk")
    across = {"blk": flip(own, 2)}
    beside = {"blk": flip(own, 1)}
    partner = [None] + [{"dp": flip(me, k)} for k in range(1, groups)]

    fetches = [
        pltpu.make_async_copy(group_hbm, ids.at[0], fetched.at[0]),
        pltpu.make_async_copy(cluster_hbm, ids.at[1], fetched.at[1]),
        pltpu.make_async_copy(order_hbm, ids.at[2], fetched.at[2]),
        pltpu.make_async_copy(emb_hbm, emb_ref, fetched.at[3]),
    ]
    for fetch in fetches:
        fetch.start()

    lead = lax.rem(own, jnp.int32(2)) == 0
    rows_of = [me] + [flip(me, k) for k in range(1, groups)]
    far_y = [{"dp": row, "blk": flip(own, 2)} for row in rows_of]
    far_c = [{"dp": row, "blk": flip(own, 1)} for row in rows_of]
    barrier = pltpu.get_barrier_semaphore()
    for who in partner[1:] + far_y + far_c:
        pl.semaphore_signal(barrier, inc=1, device_id=who, device_id_type=MESH)

    def remote(src, dst, ssem, rsem, who):
        return pltpu.make_async_remote_copy(
            src_ref=src, dst_ref=dst, send_sem=ssem, recv_sem=rsem, device_id=who, device_id_type=MESH
        )

    for fetch in fetches[:3]:
        fetch.wait()
    group = ids[0]
    combined = ids[1] * total + ids[2] + 1
    relative = jnp.bitwise_xor(group, me)
    member = lax.broadcasted_iota(jnp.int32, (groups, points), 0) == relative
    member_f = jnp.where(member, 1.0, 0.0)
    earlier = lax.broadcasted_iota(jnp.int32, (points, points), 0) < lax.broadcasted_iota(
        jnp.int32, (points, points), 1
    )
    before = jnp.dot(
        member_f.astype(jnp.bfloat16),
        jnp.where(earlier, 1.0, 0.0).astype(jnp.bfloat16),
        preferred_element_type=jnp.float32,
    )
    rank = jnp.sum(before * member_f, axis=0, keepdims=True).astype(jnp.int32)
    target = relative * cap + rank

    digits = jnp.concatenate(
        [combined & 127, (combined >> 7) & 127, combined >> 14, jnp.zeros((5, points), jnp.int32)], axis=0
    ).astype(jnp.float32).astype(jnp.bfloat16)
    lane_row = lax.broadcasted_iota(jnp.int32, (groups * LANES, points), 0)
    lane_slot = (lane_row // LANES) * cap + (lane_row & (cap - 1))
    pick = jnp.where(lane_slot == target, 1.0, 0.0).astype(jnp.bfloat16)
    got = lax.dot_general(digits, pick, NT, preferred_element_type=jnp.float32)
    row = got[0:1, :] + 128.0 * got[1:2, :] + 16384.0 * got[2:3, :]
    row = jnp.broadcast_to(row.astype(jnp.int32), (8, groups * LANES))
    meta[0, 0] = row[:, :LANES]
    for k in range(1, groups):
        msend[k] = row[:, k * LANES:(k + 1) * LANES]

    fetches[3].wait()
    values = emb_ref[...].astype(jnp.float32)
    scale = lax.rsqrt(jnp.mean(values * values, axis=1, keepdims=True) + 1e-06)
    unit = (values * scale * width ** (-0.5)).astype(jnp.bfloat16)

    pl.semaphore_wait(barrier, 3 * groups - 1)

    started = []
    meta_copies = [None] * groups
    for k in order:
        meta_copies[k] = remote(msend.at[k], meta.at[0, k], sm.at[k], rm.at[k], partner[k])
        meta_copies[k].start()

    first = [None] * groups
    over_y = [None] * groups
    over_c = [None] * groups

    def forward(k):
        over_y[k] = remote(keys.at[0, k], keys.at[2, k], sy.at[k], ry.at[k], across)
        over_y[k].start()
        over_c[k] = remote(keys.at[0, k], keys.at[1, k], sc.at[k], rc.at[k], beside)
        pl.when(jnp.logical_not(lead))(over_c[k].start)

    slot_rows = lax.broadcasted_iota(jnp.int32, (cap, points), 0)
    for k in [order[0], 0] + list(order[1:]):
        place = jnp.where(slot_rows + k * cap == target, 1.0, 0.0).astype(jnp.bfloat16)
        rows = jnp.dot(place, unit, preferred_element_type=jnp.float32).astype(jnp.bfloat16)
        if k == 0:
            keys[0, 0] = rows
            forward(0)
        else:
            send[k] = rows
            first[k] = remote(send.at[k], keys.at[0, k], s1.at[k], r1.at[k], partner[k])
            first[k].start()

    def key_rows(r):
        lane_block = lax.broadcasted_iota(jnp.int32, (1, LANES), 1) // cap
        rows = []
        for t in range(tiles):
            row = meta[r, t * per][0:1, :]
            for j in range(1, per):
                row = jnp.where(lane_block == j, meta[r, t * per + j][0:1, :], row)
            rows.append(row)
        return rows

    def key_tiles(r):
        for t, row in enumerate(key_rows(r)):
            kmeta[r, t] = jnp.broadcast_to(row, (LANES, LANES)).T

    for k in order:
        meta_copies[k].wait_recv()
    meta_y = remote(meta.at[0], meta.at[2], smx.at[0], rmx.at[0], across)
    meta_y.start()
    meta_c = remote(meta.at[0], meta.at[1], smx.at[1], rmx.at[1], beside)
    meta_c.start()
    key_tiles(0)
    best[...] = jnp.full_like(best, -2.0)

    middle, half = groups // 2, tiles // 2
    both, near, far = (0, tiles), (0, half), (half, tiles)

    def visit(q, r, q_span, r_span):
        (q0, q1), (r0, r1) = q_span, r_span
        wide = (q1 - q0) * LANES
        queries = keys[q, q0 * per:q1 * per].reshape(wide, width)
        query = jnp.concatenate(key_rows(q)[q0:q1], axis=1)
        floor = (query - 1) & (-total)
        found = best[q, :, q0 * LANES:q1 * LANES]
        for t0 in range(r0, r1, half):
            block = keys[r, t0 * per:(t0 + half) * per].reshape(half * LANES, width)
            scores = lax.dot_general(block, queries, NT, preferred_element_type=jnp.float32)
            for t in range(half):
                mine = jnp.concatenate([kmeta[r, t0 + t]] * (q1 - q0), axis=1)
                part = jnp.where((mine < query) & (mine > floor), scores[t * LANES:(t + 1) * LANES], -2.0)
                found = jnp.maximum(found, jnp.max(part.reshape(LANES // 8, 8, wide), axis=0))
        best[q, :, q0 * LANES:q1 * LANES] = found

    def answer(q):
        found = jnp.max(best[q], axis=0, keepdims=True)
        found = jnp.broadcast_to(found, (8, slots))
        for t in range(tiles):
            res[q, t] = found[:, t * LANES:(t + 1) * LANES]

    for k in order:
        first[k].wait_recv()
        forward(k)
        if k == middle - 1:
            meta_y.wait_recv()
            key_tiles(2)
            meta_c.wait_recv()
            key_tiles(1)
            visit(0, 0, near, near)
    visit(0, 0, far, near)
    visit(0, 0, both, far)

    @pl.when(lead)
    def _():
        for k in range(middle):
            over_c[k].wait_recv()
        visit(1, 0, near, both)
        visit(0, 1, both, near)

    for k in range(middle):
        over_y[k].wait_recv()
    visit(0, 2, both, near)

    @pl.when(lead)
    def _():
        visit(2, 1, near, near)
        visit(1, 2, near, near)
        for k in range(middle, groups):
            over_c[k].wait_recv()
        visit(1, 0, far, both)
        visit(0, 1, both, far)
        visit(2, 1, near, far)
        visit(1, 2, far, near)

    for k in range(middle, groups):
        over_y[k].wait_recv()

    extra_y = [remote(res.at[2, k // per], back.at[1, k], s2.at[k], r2.at[k], far_y[k]) for k in range(groups)]
    extra_c = [remote(res.at[1, k // per], back.at[1, k], s3.at[k], r2.at[k], far_c[k]) for k in range(groups)]

    @pl.when(lead)
    def _():
        visit(2, 1, far, both)
        answer(2)
        for copy in extra_y:
            copy.start()
        visit(1, 2, both, far)
        answer(1)
        for copy in extra_c:
            copy.start()

    visit(0, 2, both, far)
    answer(0)
    back[0, 0] = res[0, 0]
    replies = [None] * groups
    for k in order:
        replies[k] = remote(res.at[0, k // per], back.at[0, k], sb.at[k], rb.at[k], partner[k])
        replies[k].start()

    for k in range(groups):
        over_y[k].wait_send()
        if k:
            first[k].wait_send()
            meta_copies[k].wait_send()
    meta_y.wait_send()
    meta_c.wait_send()

    @pl.when(jnp.logical_not(lead))
    def _():
        for k in range(groups):
            over_c[k].wait_send()

    lane_block = lax.broadcasted_iota(jnp.int32, (1, LANES), 1) // cap
    nearest = jnp.full((1, points), -2.0, jnp.float32)
    slot_iota = lax.broadcasted_iota(jnp.int32, (LANES, points), 0)
    for t in range(tiles):
        for j in range(per):
            if t * per + j:
                replies[t * per + j].wait_recv()
            extra_y[t * per + j].wait_recv()
        row = jnp.maximum(back[0, t * per], back[1, t * per])[0:1, :]
        for j in range(1, per):
            pair = jnp.maximum(back[0, t * per + j], back[1, t * per + j])
            row = jnp.where(lane_block == j, pair[0:1, :], row)
        column = jnp.broadcast_to(row, (LANES, LANES)).T
        column = jnp.concatenate([column] * (points // LANES), axis=1)
        hit = jnp.where(slot_iota + t * LANES == target, column, -2.0)
        nearest = jnp.maximum(nearest, jnp.max(hit, axis=0, keepdims=True))
    out_ref[...] = jnp.where(nearest > -1.5, nearest, -1.0).reshape(points)
    for k in order:
        replies[k].wait_send()

    @pl.when(lead)
    def _():
        for k in range(groups):
            extra_y[k].wait_send()
            extra_c[k].wait_send()


def body(total, embeddings, point_group, point_cluster, point_order):
    groups = lax.axis_size("dp")
    blocks = lax.axis_size("blk")
    points, width = embeddings.shape
    cap = 2 * points // groups
    slots = groups * cap
    near, far = list(range(1, groups // 2)), list(range(groups // 2, groups))
    order = [k for pair in zip(near, far) for k in pair] + far[len(near):]
    dma = pltpu.SemaphoreType.DMA
    out = pl.pallas_call(
        functools.partial(kernel, groups, total, order),
        out_shape=jax.ShapeDtypeStruct((points,), jnp.float32),
        in_specs=[pl.BlockSpec(memory_space=pl.ANY)] * 4,
        out_specs=pl.BlockSpec(memory_space=pltpu.VMEM),
        scratch_shapes=[
            pltpu.VMEM((points, width), jnp.bfloat16),
            pltpu.VMEM((3, 1, points), jnp.int32),
            dma((4,)),
            pltpu.VMEM((groups, cap, width), jnp.bfloat16),
            pltpu.VMEM((3, groups, cap, width), jnp.bfloat16),
            pltpu.VMEM((groups, 8, LANES), jnp.int32),
            pltpu.VMEM((3, groups, 8, LANES), jnp.int32),
            pltpu.VMEM((3, slots // LANES, LANES, LANES), jnp.int32),
            pltpu.VMEM((3, 8, slots), jnp.float32),
            pltpu.VMEM((3, slots // LANES, 8, LANES), jnp.float32),
            pltpu.VMEM((2, groups, 8, LANES), jnp.float32),
        ]
        + [dma((groups,))] * 8
        + [dma((2,))] * 2
        + [dma((groups,))] * 5,
        compiler_params=pltpu.CompilerParams(
            collective_id=0, has_side_effects=True, vmem_limit_bytes=64 * 1024 * 1024 - 65536
        ),
        cost_estimate=pl.CostEstimate(
            flops=2 * slots * slots * blocks * width, bytes_accessed=points * width * 2, transcendentals=points
        ),
    )(embeddings, point_group.reshape(1, points), point_cluster.reshape(1, points), point_order.reshape(1, points))
    return out


def solution(mesh):
    in_specs = (P(("dp", "blk"), None), P(("dp", "blk"), None), P(("dp", "blk")), P(("dp", "blk")))
    out_specs = P(("dp", "blk"))

    def run(embeddings, point_group, point_cluster, point_order):
        inner = functools.partial(body, embeddings.shape[0])
        return jax.shard_map(inner, mesh=mesh, in_specs=in_specs, out_specs=out_specs, check_vma=False)(
            embeddings, point_group, point_cluster, point_order
        )

    return run
```
